32 devices in a mesh: panel: 8 (over z, y), feat: 4 (over x, core).
Axes of the slice: x: 2, y: 2, z: 4, core: 2. Of those that a mesh axis runs over, the one named last changes fastest.
Arguments:
- dosage: bfloat16 [7168, 4096], P('panel', 'feat'), may hold values from 0 to 1, as said below
- row_counts: int32 [8], P('panel'), may hold values from 0 to 896, as said below
- assignment: int32 [7168], P('panel'), may hold values from 0 to 7, as said below
- center: float32 [4096], replicated, may hold values from 0.06 to 0.54
- weight: float32 [4096], replicated, may hold values from 0.5 to 2
Outputs:
- kinship: float32 [4096, 4, 512], P('panel', None, 'feat')
The draws below stay inside these ranges and needn't reach their ends.
Inputs may be any that keep to these rules, and one draw needn't show every extreme that they name: Batch b has row_counts[b] live rows; some batch has exactly 896 in every draw. `assignment`: over all batches each panel receives exactly 512 live rows; one batch sends at most 112 live rows to one panel, and some batch sends exactly 112 to every panel in every draw. Entries of rows that are not live are ignored. `dosage`: zero where a k-mer is absent.
All inputs are finite; a program needn't handle non-finite values.
Results may differ from the reference program's by a relative error of at most 0.004.
Values may be sent and summed in bfloat16 or wider, within the bound.
No kernel may reach another device: no remote copies, remote signals or barrier semaphores. Data moves between devices by JAX's collectives and lax.ppermute only.
A program may use at most 64 MiB of HBM per device.

```python
import math
import jax
import jax.numpy as jnp
from jax import lax

F = 4096
P_SIZE = 512
ROUNDS = 4
BATCHES = 8
PAIR_ROWS = 128
CAP = 896
SAMPLES = 4096
N_PANEL = 8


def presence_rates(key):
    return jax.random.uniform(jax.random.fold_in(key, 29), (F,), jnp.float32, 0.1, 0.6)


def routing_matrix(key):
    base_key = jax.random.fold_in(key, 17)
    half_count = BATCHES // 2
    low_rows = PAIR_ROWS // 8
    top_rows = PAIR_ROWS - low_rows
    levels = jax.random.randint(jax.random.fold_in(base_key, 1), (half_count,), low_rows, top_rows + 1)
    jitter = jax.random.randint(jax.random.fold_in(base_key, 2), (half_count, BATCHES), -1, 2)
    first_rows = jnp.clip(levels[:, None] + jitter, low_rows, top_rows)
    chosen = jax.random.randint(jax.random.fold_in(base_key, 3), (), 0, half_count)
    first_rows = jnp.where(jnp.arange(half_count)[:, None] == chosen, top_rows, first_rows)
    return jnp.stack([first_rows, PAIR_ROWS - first_rows], axis=1).reshape(BATCHES, BATCHES).astype(jnp.int32)


def draw_row_counts(key, part):
    return jnp.sum(routing_matrix(key), axis=1).astype(jnp.int32)


def draw_assignment(key, part):
    routed = routing_matrix(key)
    boundary = jnp.cumsum(routed, axis=1)
    slot_ids = jnp.arange(CAP, dtype=jnp.int32)
    targets = jnp.sum((boundary[:, None, :] <= slot_ids[None, :, None]).astype(jnp.int32), axis=2)
    alive = slot_ids[None, :] < boundary[:, -1:]
    scores = jax.random.randint(jax.random.fold_in(key, 41), (BATCHES, CAP), 0, 65536) * CAP + slot_ids[None, :]
    scores = jnp.where(alive, scores, 65536 * CAP + slot_ids[None, :])
    ordering = jnp.argsort(scores, axis=1, stable=True)
    shuffled = jnp.take_along_axis(targets, ordering, axis=1)
    filler = jax.random.randint(jax.random.fold_in(key, 43), (BATCHES, CAP), 0, BATCHES)
    return jnp.where(alive, shuffled, filler).reshape(BATCHES * CAP).astype(jnp.int32)


def draw_dosage(key, part):
    rates = presence_rates(key)
    uniform_draw = jax.random.uniform(jax.random.fold_in(key, 31), (BATCHES * CAP, F), jnp.float32)
    present = uniform_draw < rates[None, :]
    scaled = uniform_draw / rates[None, :]
    confidence = 0.5 + 0.5 * scaled
    return jnp.where(present, confidence, 0.0).astype(jnp.bfloat16)


def draw_center(key, part):
    rates = presence_rates(key)
    spread = jax.random.uniform(jax.random.fold_in(key, 37), (F,), jnp.float32, 0.8, 1.2)
    return (0.75 * rates * spread).astype(jnp.float32)


def setup_inputs(seed: int = 0) -> dict:
    key_list = jax.random.split(jax.random.key(seed), 6)
    dosage = draw_dosage(jax.random.fold_in(key_list[5], 71), 0)
    row_counts = draw_row_counts(jax.random.fold_in(key_list[5], 71), 0)
    assignment = draw_assignment(jax.random.fold_in(key_list[5], 71), 0)
    center = draw_center(jax.random.fold_in(key_list[5], 71), 0)
    weight = jnp.clip(jnp.exp(jax.random.uniform(key_list[4], (F,), jnp.float32, math.log(0.5), math.log(2.0))), 0.5, 2.0)
    return {"dosage": dosage, "row_counts": row_counts, "assignment": assignment, "center": center, "weight": weight}


def reference(dosage, row_counts, assignment, center, weight):
    rows_batch = dosage.reshape(BATCHES, CAP, F)
    standard = lax.map(lambda block: ((block.astype(jnp.float32) - center) * weight).astype(jnp.bfloat16), rows_batch)
    targets = assignment.reshape(BATCHES, CAP).astype(jnp.int32)
    alive = jnp.arange(CAP, dtype=jnp.int32)[None, :] < row_counts[:, None]
    onehot = ((targets[:, :, None] == jnp.arange(N_PANEL, dtype=jnp.int32)[None, None, :]) & alive[:, :, None]).astype(jnp.int32)
    per_batch = lax.optimization_barrier(jnp.sum(onehot, axis=1))
    offsets = jnp.cumsum(per_batch, axis=0) - per_batch
    earlier = lax.optimization_barrier(jnp.sum((jnp.cumsum(onehot, axis=1) - onehot) * onehot, axis=2))
    before = jnp.take_along_axis(offsets, targets, axis=1)
    positions = jnp.where(alive, targets * P_SIZE + before + earlier, SAMPLES).astype(jnp.int32)
    panels = jnp.zeros((SAMPLES, F), jnp.bfloat16).at[positions.reshape(-1)].set(standard.reshape(-1, F), mode='drop')
    panel_grid = panels.reshape(N_PANEL, P_SIZE, F)
    tile_scale = 1.0 / math.sqrt(F)

    def one_panel(panel_index):
        own_rows = panel_grid[panel_index].astype(jnp.float32)
        partner_ids = ((panel_index - 1 - jnp.arange(ROUNDS, dtype=jnp.int32)) % N_PANEL).astype(jnp.int32)
        partner_rows = panel_grid[partner_ids].astype(jnp.float32)
        return jnp.einsum('af,rcf->arc', own_rows, partner_rows) * tile_scale
    tiles = lax.map(one_panel, jnp.arange(N_PANEL, dtype=jnp.int32))
    return tiles.reshape(SAMPLES, ROUNDS, P_SIZE)
```

```python
import functools
import math

import jax
import jax.numpy as jnp
from jax import lax
from jax.experimental import pallas as pl
from jax.experimental.pallas import tpu as pltpu
from jax.sharding import PartitionSpec as P

F = 4096
P_SIZE = 512
ROUNDS = 4
PAIR_ROWS = 128
NZ, NY, NX, NC = 4, 2, 2, 2
VMEM_LIMIT = 40 * 1024 * 1024
BOTH = ("panel", "feat")
ORDER = ((2, 3, 1, 0), (0, 3, 2, 1), (3, 2, 1, 0), (0, 3, 1, 2))
CHUNKS = ((0,), (1,), (2, 3))
FOUND = (
    {1: {0: "a0", 3: "a1", 2: "a2"}, 2: {3: "a3", 0: "d0", 2: "d2"}, 3: {0: "e0", 3: "e1", 2: "e2"}},
    {
        0: {2: "a0", 3: "a1", 1: "a2", 0: "a3"},
        2: {3: "b0", 2: "b1", 1: "b2", 0: "b3"},
        3: {0: "c0", 3: "c1", 1: "c2", 2: "c3"},
    },
    {
        3: {0: "a0", 3: "a1", 1: "a2", 2: "a3"},
        1: {0: "b0", 3: "b1", 2: "b2", 1: "b3"},
        0: {2: "c0", 3: "c1", 1: "c2", 0: "c3"},
    },
    {2: {3: "a0", 2: "a1", 1: "a2"}, 1: {3: "a3", 2: "d0", 1: "d2"}, 0: {2: "e0", 3: "e1", 1: "e2"}},
)


def shifted(value, axis, steps):
    count = lax.axis_size(axis)
    pairs = [(source, (source + steps) % count) for source in range(count)]
    return lax.ppermute(value, axis, pairs)


def tile_of(left_rows, partner):
    return lax.dot_general(
        left_rows, partner, (((1,), (1,)), ((), ())), preferred_element_type=jnp.float32
    )


def general_shards(dosage, row_counts, assignment, center, weight):
    panel_total = lax.axis_size("panel")
    feat_index = lax.axis_index("feat")
    capacity = dosage.shape[0]
    feat_width = dosage.shape[1]
    send_rows = capacity // panel_total
    feat_start = feat_index * feat_width
    center_part = lax.dynamic_slice_in_dim(center, feat_start, feat_width)
    weight_part = lax.dynamic_slice_in_dim(weight, feat_start, feat_width)
    standard = ((dosage.astype(jnp.float32) - center_part) * weight_part).astype(jnp.bfloat16)
    slot_ids = jnp.arange(capacity, dtype=jnp.int32)
    live_rows = slot_ids < row_counts[0]
    targets = jnp.arange(panel_total, dtype=jnp.int32)
    onehot = ((assignment[:, None] == targets[None, :]) & live_rows[:, None]).astype(jnp.int32)
    earlier = jnp.sum((jnp.cumsum(onehot, axis=0) - onehot) * onehot, axis=1)
    slot_index = jnp.where(live_rows, assignment * send_rows + earlier, panel_total * send_rows)
    outgoing = (
        jnp.zeros((panel_total * send_rows, feat_width), jnp.bfloat16)
        .at[slot_index]
        .set(standard, mode="drop")
    )
    outgoing = outgoing.reshape(panel_total, send_rows, feat_width)
    sent_counts = jnp.sum(onehot, axis=0).reshape(panel_total, 1)
    incoming, arrived = (
        lax.all_to_all(outgoing, "panel", split_axis=0, concat_axis=0, tiled=True),
        lax.all_to_all(sent_counts, "panel", split_axis=0, concat_axis=0, tiled=True),
    )
    arrived_rows = arrived[:, 0]
    offsets = jnp.cumsum(arrived_rows) - arrived_rows
    within = jnp.arange(send_rows, dtype=jnp.int32)
    positions = jnp.where(
        within[None, :] < arrived_rows[:, None], offsets[:, None] + within[None, :], P_SIZE
    )
    own_panel = (
        jnp.zeros((P_SIZE, feat_width), jnp.bfloat16)
        .at[positions.reshape(-1)]
        .set(incoming.reshape(-1, feat_width), mode="drop")
    )
    tile_scale = 1.0 / math.sqrt(F)
    partners = []
    for round_index in range(ROUNDS):
        partners.append(shifted(own_panel, "panel", round_index + 1))
    kinship = (
        jnp.concatenate(
            [
                lax.psum_scatter(
                    tile_of(own_panel, partner)[:, None, :], "feat", scatter_dimension=2, tiled=True
                )
                for partner in partners
            ],
            axis=1,
        )
        * tile_scale
    )
    return kinship


def hop(value, move):
    pairs = []
    for z in range(NZ):
        for y in range(NY):
            for x in range(NX):
                for c in range(NC):
                    to = move(z, y, x, c)
                    if to is not None:
                        tz, ty, tx, tc = to
                        pairs.append((((z * 2 + y) * 2 + x) * 2 + c, ((tz * 2 + ty) * 2 + tx) * 2 + tc))
    return lax.ppermute(value, BOTH, pairs)


def to_y(value):
    return hop(value, lambda z, y, x, c: (z, 1 - y, x, c))


def to_x(value):
    return hop(value, lambda z, y, x, c: (z, y, 1 - x, c))


def to_diagonal(value):
    return hop(value, lambda z, y, x, c: (z, 1 - y, 1 - x, c))


def to_core(value):
    return hop(value, lambda z, y, x, c: (z, y, x, 1 - c))


def z_ends(value):
    return hop(value, lambda z, y, x, c: (z ^ 1, y, x, c))


def z_middle(value):
    return hop(value, lambda z, y, x, c: (3 - z, y, x, c) if z in (1, 2) else None)


def place():
    panel, feat = lax.axis_index("panel"), lax.axis_index("feat")
    return panel // NY, panel % NY, feat // NC, feat % NC


def call(kernel, out_shape, in_specs, out_specs, cost, scratch=()):
    return pl.pallas_call(
        kernel,
        name=kernel.func.__name__,
        out_shape=out_shape,
        in_specs=in_specs,
        out_specs=out_specs,
        scratch_shapes=scratch,
        compiler_params=pltpu.CompilerParams(vmem_limit_bytes=VMEM_LIMIT),
        cost_estimate=pl.CostEstimate(flops=cost[0], bytes_accessed=cost[1], transcendentals=0),
    )


IN_VMEM = pl.BlockSpec(memory_space=pltpu.VMEM)
IN_SMEM = pl.BlockSpec(memory_space=pltpu.SMEM)
ANYWHERE = pl.BlockSpec(memory_space=pl.ANY)
IN_HBM = pl.BlockSpec(memory_space=pltpu.HBM)


def bf16(*shape):
    return jax.ShapeDtypeStruct(shape, jnp.bfloat16)


def group_at(step):
    z, _, _, _ = place()
    group = jnp.int32(ORDER[0][step])
    for plane in range(1, NZ):
        group = jnp.where(z == plane, ORDER[plane][step], group)
    return group


def picks(slot, slots, step):
    group_rows = 2 * slots
    row = lax.broadcasted_iota(jnp.int32, (group_rows, slot.shape[1]), 0) + group_at(step) * group_rows
    return jnp.where(row == slot, 1.0, 0.0).astype(jnp.bfloat16)


def picked(pick, rows):
    return jnp.dot(pick, rows, preferred_element_type=jnp.float32).astype(jnp.bfloat16)


def columns_of_half(width, part):
    half = width // NY
    feat = lax.axis_index("feat")
    return (
        pl.ds(pl.multiple_of(part * half, half), half),
        pl.ds(pl.multiple_of(feat * width + part * half, half), half),
    )


def standard(dosage_ref, center_ref, weight_ref, part):
    columns, features = columns_of_half(dosage_ref.shape[1], part)
    rows = dosage_ref[:, columns].astype(jnp.float32)
    return ((rows - center_ref[:, features]) * weight_ref[:, features]).astype(jnp.bfloat16)


def first_kernel(
    slots, count_ref, assign_ref, center_ref, weight_ref, dosage_ref, slot_ref, counts_ref, rows_ref, away_ref
):
    capacity = dosage_ref.shape[0]
    _, y, _, _ = place()
    panels = capacity // slots
    assign = assign_ref[...]
    lane = lax.broadcasted_iota(jnp.int32, (panels, capacity), 1)
    panel_id = lax.broadcasted_iota(jnp.int32, (panels, capacity), 0)
    live = lane < count_ref[0]
    member = (panel_id == assign) & live
    running = member.astype(jnp.int32)
    step = 1
    while step < capacity:
        running = running + jnp.where(lane >= step, pltpu.roll(running, step, 1), 0)
        step *= 2
    counts_ref[...] = jnp.broadcast_to(running[:, capacity - 1 :], counts_ref.shape)
    rank = jnp.sum(jnp.where(member, running - 1, 0), axis=0, keepdims=True)
    slot = jnp.where(live[:1], assign * slots + rank, -1)
    slot_ref[...] = slot
    rows_ref[...] = standard(dosage_ref, center_ref, weight_ref, 1 - y)
    at = 0
    for step in CHUNKS[0]:
        away_ref[pl.ds(at, 2 * slots), :] = picked(picks(slot, slots, step), rows_ref[...])
        at += 2 * slots


def rest_kernel(slots, slot_ref, rows_ref, center_ref, weight_ref, dosage_ref, own_ref, *away_refs):
    _, y, _, _ = place()
    group_rows = 2 * slots
    slot = slot_ref[...]
    pick = {}
    for chunk, away_ref in zip(CHUNKS[1:], away_refs):
        for k, step in enumerate(chunk):
            pick[step] = picks(slot, slots, step)
            away_ref[pl.ds(k * group_rows, group_rows), :] = picked(pick[step], rows_ref[...])
    stay = standard(dosage_ref, center_ref, weight_ref, y)
    for step in range(NZ):
        rows = pick[step] if step in pick else picks(slot, slots, step)
        own_ref[pl.ds(step * group_rows, group_rows), :] = picked(rows, stay)


def merge_kernel(slots, chunk, counts_ref, own_ref, other_ref, *out_refs):
    _, y, _, _ = place()
    row = lax.broadcasted_iota(jnp.int32, (PAIR_ROWS, slots), 0)
    slot = lax.broadcasted_iota(jnp.int32, (PAIR_ROWS, slots), 1)
    for at, (step, out_ref) in enumerate(zip(chunk, out_refs)):
        group = group_at(step)
        for k in range(2):
            n_own = counts_ref[group * 2 + k, 0]
            n_other = PAIR_ROWS - n_own
            own_at = jnp.where(y == 0, 0, n_other)
            other_at = jnp.where(y == 0, n_own, 0)
            pick_own = jnp.where((row == slot + own_at) & (slot < n_own), 1.0, 0.0).astype(jnp.bfloat16)
            pick_other = jnp.where((row == slot + other_at) & (slot < n_other), 1.0, 0.0).astype(jnp.bfloat16)
            merged = jnp.dot(
                pick_own, own_ref[pl.ds((step * 2 + k) * slots, slots), :], preferred_element_type=jnp.float32
            ) + jnp.dot(
                pick_other, other_ref[pl.ds((at * 2 + k) * slots, slots), :], preferred_element_type=jnp.float32
            )
            out_ref[pl.ds(k * PAIR_ROWS, PAIR_ROWS), :] = merged.astype(jnp.bfloat16)


def collect_kernel(names, whole, split, *refs):
    pieces = dict(zip(names, refs))
    send_ref, keep_ref, sems = refs[len(names) :]
    z, _, _, c = place()
    for zz in range(NZ):
        for cc in range(NC):

            @pl.when((z == zz) & (c == cc))
            def _(zz=zz, cc=cc):
                copies = []
                sent = kept = 0
                for r in whole + split:
                    g = (zz - r) % NZ
                    for s in range(NZ):
                        source = pieces["o%d" % ORDER[zz].index(g) if s == zz else FOUND[zz][s][g]]
                        if r in split and s % NC == cc:
                            copies.append((source, keep_ref.at[kept]))
                            kept += 1
                        else:
                            copies.append((source, send_ref.at[sent]))
                            sent += 1
                started = []
                for i, (source, target) in enumerate(copies):
                    copy = pltpu.make_async_copy(source, target, sems.at[i])
                    copy.start()
                    started.append(copy)
                for copy in started:
                    copy.wait()


def tile_kernel(tiles, n_kept, *refs):
    own_ref, own_far_ref = refs[:2]
    kept_refs = refs[2 : 2 + n_kept]
    far_refs = refs[2 + n_kept : 2 + 2 * n_kept]
    mine_ref, x_ref, y_ref, d_ref = refs[2 + 2 * n_kept :]
    _, y, x, c = place()
    depth = own_ref.shape[2]
    nt = (((1,), (1,)), ((), ()))

    def rows_of(ref, p):
        return ref[0:NZ, pl.ds(p * PAIR_ROWS, PAIR_ROWS), :].reshape(P_SIZE, depth)

    def columns_of(distance, q, part, near):
        rows = pl.ds(q * PAIR_ROWS, PAIR_ROWS)
        if distance == 0:
            return (own_ref if near else own_far_ref)[2 * part + c, rows, :]
        if near:
            return kept_refs[distance - 1][part, rows, :]
        ref = far_refs[distance - 1]
        first = ref.shape[0] - 2
        return ref[first + part, rows, :]

    for p in range(2):
        left, left_far = rows_of(own_ref, p), rows_of(own_far_ref, p)
        for part in range(2):
            near = jnp.concatenate([columns_of(d, q, part, True) for d, q in tiles[p]], axis=0)
            far = jnp.concatenate([columns_of(d, q, part, False) for d, q in tiles[p]], axis=0)
            total = lax.dot_general(left, near, nt, preferred_element_type=jnp.float32) + lax.dot_general(
                left_far, far, nt, preferred_element_type=jnp.float32
            )

            @pl.when((y == p) & (x == part))
            def _(total=total):
                mine_ref[...] = total

            @pl.when((y == p) & (x != part))
            def _(total=total):
                x_ref[...] = total.astype(jnp.bfloat16)

            @pl.when((y != p) & (x == part))
            def _(total=total):
                y_ref[...] = total.astype(jnp.bfloat16)

            @pl.when((y != p) & (x != part))
            def _(total=total):
                d_ref[...] = total.astype(jnp.bfloat16)


def plane_tiles(tiles, own, own_far, kept, far):
    columns = len(tiles[0]) * PAIR_ROWS
    part = bf16(P_SIZE, columns)
    mine, x_part, y_part, d_part = call(
        functools.partial(tile_kernel, tiles, len(kept)),
        (jax.ShapeDtypeStruct((P_SIZE, columns), jnp.float32), part, part, part),
        [IN_VMEM] * (2 + 2 * len(kept)),
        (IN_VMEM,) * 4,
        (2 * 4 * P_SIZE * columns * 2 * own.shape[2], 8 * 1024 * 1024),
    )(own, own_far, *kept, *far)
    return mine, to_y(y_part), to_diagonal(d_part), to_x(x_part)


def plane_shards(dosage, row_counts, assignment, center, weight):
    capacity, width = dosage.shape
    half = width // NY
    panels = NZ * NY
    slots = capacity // panels
    group_slots = 2 * slots
    group_rows = 2 * PAIR_ROWS

    center, weight = center.reshape(1, -1), weight.reshape(1, -1)
    chunk_rows = [len(chunk) * group_slots for chunk in CHUNKS]
    slot, counts, rows, away = call(
        functools.partial(first_kernel, slots),
        (
            jax.ShapeDtypeStruct((1, capacity), jnp.int32),
            jax.ShapeDtypeStruct((panels, 128), jnp.int32),
            bf16(capacity, half),
            bf16(chunk_rows[0], half),
        ),
        [IN_SMEM] + [IN_VMEM] * 4,
        (IN_VMEM,) * 4,
        (2 * chunk_rows[0] * capacity * half, 3 * capacity * width),
    )(row_counts, assignment.reshape(1, capacity), center, weight, dosage)
    with jax.named_scope("y0"):
        came = [to_y(away)]
    own, *later = call(
        functools.partial(rest_kernel, slots),
        (bf16(capacity, half),) + tuple(bf16(n, half) for n in chunk_rows[1:]),
        [IN_VMEM] * 5,
        (IN_VMEM,) * len(CHUNKS),
        (2 * capacity * capacity * width, 3 * capacity * width),
    )(slot, rows, center, weight, dosage)
    for k, away in enumerate(later):
        with jax.named_scope("y%d" % (k + 1)):
            if k >= 1:
                away, _ = lax.optimization_barrier((away, came[k - 1]))
            came.append(to_y(away))
    pieces = {}
    for chunk, other in zip(CHUNKS, came):
        merged = call(
            functools.partial(merge_kernel, slots, chunk),
            (bf16(group_rows, half),) * len(chunk),
            [IN_SMEM, IN_VMEM, IN_VMEM],
            (IN_VMEM,) * len(chunk),
            (2 * len(chunk) * group_rows * group_slots * half, 4 * group_rows * half * 2),
        )(counts, own, other)
        for step, piece in zip(chunk, merged):
            pieces["o%d" % step] = piece

    z = lax.axis_index("panel") // NY

    def either(first, second, planes):
        return jnp.where((z == planes[0]) | (z == planes[1]), pieces[first], pieces[second])

    def ends(name, value):
        with jax.named_scope(name):
            pieces[name] = z_ends(value)

    def middle(name, value):
        with jax.named_scope(name):
            pieces[name] = z_middle(value)

    for k in range(NZ - 1):
        ends("a%d" % k, pieces["o%d" % k])
        middle("b%d" % k, pieces["o%d" % k])
    pieces["f"] = either("b0", "b1", (0, 1))
    ends("a3", either("o3", "f", (0, 3)))
    middle("b3", pieces["o3"])
    ends("d0", either("b3", "b2", (0, 1)))
    for k in range(NZ):
        middle("c%d" % k, pieces["a%d" % k])
    ends("e0", pieces["c0"])
    ends("e1", pieces["c1"])
    ends("d2", either("b1", "b3", (0, 1)))
    ends("e2", either("c3", "c2", (0, 1)))

    def collect(whole, split):
        sent, kept = 4 * len(whole) + 2 * len(split), 2 * len(split)
        names = set()
        for z in range(NZ):
            for r in whole + split:
                g = (z - r) % NZ
                names.add("o%d" % ORDER[z].index(g))
                names.update(FOUND[z][s][g] for s in range(NZ) if s != z)
        names = sorted(names)
        return call(
            functools.partial(collect_kernel, names, whole, split),
            (bf16(sent, group_rows, half), bf16(kept, group_rows, half)),
            [ANYWHERE] * len(names),
            (ANYWHERE, ANYWHERE),
            (0, 4 * (sent + kept) * group_rows * half),
            (pltpu.SemaphoreType.DMA((sent + kept,)),),
        )(*[pieces[name] for name in names])

    sent1, kept1 = collect((0,), (1,))
    far1 = to_core(sent1)
    first = plane_tiles((((1, 1), (1, 0)), ((0, 0), (1, 1))), sent1, far1, (kept1,), (far1,))
    sent2, kept2 = collect((), (2,))
    far2 = to_core(sent2)
    second = plane_tiles((((2, 1), (2, 0)), ((1, 0), (2, 1))), sent1, far1, (kept1, kept2), (far1, far2))

    def total(parts):
        mine, *others = parts
        for other in others:
            mine = mine + other.astype(jnp.float32)
        return mine.reshape(P_SIZE, 2, PAIR_ROWS)

    return jnp.concatenate([total(first), total(second)], axis=1) * (1.0 / math.sqrt(F))


def solution(mesh):
    in_specs = (P("panel", "feat"), P("panel"), P("panel"), P(), P())
    out_specs = P("panel", None, "feat")
    planes = mesh.shape["panel"] == NZ * NY and mesh.shape["feat"] == NX * NC
    shards = plane_shards if planes else general_shards
    return jax.shard_map(shards, mesh=mesh, in_specs=in_specs, out_specs=out_specs, check_vma=False)
```

```python
import functools
import math

import jax
import jax.numpy as jnp
from jax import lax
from jax.experimental import pallas as pl
from jax.experimental.pallas import tpu as pltpu
from jax.sharding import PartitionSpec as P

F = 4096
P_SIZE = 512
ROUNDS = 4
PAIR_ROWS = 128
NZ, NY, NX, NC = 4, 2, 2, 2
WINDOW = 9
VMEM_LIMIT = 40 * 1024 * 1024
FIRST_LIMIT = 62 * 1024 * 1024
BOTH = ("panel", "feat")
ORDER = ((2, 3, 0, 1), (3, 2, 0, 1), (3, 2, 1, 0), (0, 3, 1, 2))
CHUNKS = ((0,), (1,), (2, 3))
FOUND = (
    {1: {3: "a0", 2: "a1", 0: "a2"}, 2: {3: "a3", 2: "d0", 0: "d1"}, 3: {0: "e0", 3: "e1", 2: "e2"}},
    {
        0: {2: "a0", 3: "a1", 0: "a2", 1: "a3"},
        2: {3: "b0", 2: "b1", 1: "b2", 0: "b3"},
        3: {0: "c0", 3: "c1", 1: "c2", 2: "c3"},
    },
    {
        3: {0: "a0", 3: "a1", 1: "a2", 2: "a3"},
        1: {3: "b0", 2: "b1", 0: "b2", 1: "b3"},
        0: {2: "c0", 3: "c1", 0: "c2", 1: "c3"},
    },
    {2: {3: "a0", 2: "a1", 1: "a2"}, 1: {3: "a3", 2: "d0", 1: "d1"}, 0: {2: "e0", 3: "e1", 1: "e2"}},
)


def shifted(value, axis, steps):
    count = lax.axis_size(axis)
    pairs = [(source, (source + steps) % count) for source in range(count)]
    return lax.ppermute(value, axis, pairs)


def tile_of(left_rows, partner):
    return lax.dot_general(
        left_rows, partner, (((1,), (1,)), ((), ())), preferred_element_type=jnp.float32
    )


def general_shards(dosage, row_counts, assignment, center, weight):
    panel_total = lax.axis_size("panel")
    feat_index = lax.axis_index("feat")
    capacity = dosage.shape[0]
    feat_width = dosage.shape[1]
    send_rows = capacity // panel_total
    feat_start = feat_index * feat_width
    center_part = lax.dynamic_slice_in_dim(center, feat_start, feat_width)
    weight_part = lax.dynamic_slice_in_dim(weight, feat_start, feat_width)
    standard = ((dosage.astype(jnp.float32) - center_part) * weight_part).astype(jnp.bfloat16)
    slot_ids = jnp.arange(capacity, dtype=jnp.int32)
    live_rows = slot_ids < row_counts[0]
    targets = jnp.arange(panel_total, dtype=jnp.int32)
    onehot = ((assignment[:, None] == targets[None, :]) & live_rows[:, None]).astype(jnp.int32)
    earlier = jnp.sum((jnp.cumsum(onehot, axis=0) - onehot) * onehot, axis=1)
    slot_index = jnp.where(live_rows, assignment * send_rows + earlier, panel_total * send_rows)
    outgoing = (
        jnp.zeros((panel_total * send_rows, feat_width), jnp.bfloat16)
        .at[slot_index]
        .set(standard, mode="drop")
    )
    outgoing = outgoing.reshape(panel_total, send_rows, feat_width)
    sent_counts = jnp.sum(onehot, axis=0).reshape(panel_total, 1)
    incoming, arrived = (
        lax.all_to_all(outgoing, "panel", split_axis=0, concat_axis=0, tiled=True),
        lax.all_to_all(sent_counts, "panel", split_axis=0, concat_axis=0, tiled=True),
    )
    arrived_rows = arrived[:, 0]
    offsets = jnp.cumsum(arrived_rows) - arrived_rows
    within = jnp.arange(send_rows, dtype=jnp.int32)
    positions = jnp.where(
        within[None, :] < arrived_rows[:, None], offsets[:, None] + within[None, :], P_SIZE
    )
    own_panel = (
        jnp.zeros((P_SIZE, feat_width), jnp.bfloat16)
        .at[positions.reshape(-1)]
        .set(incoming.reshape(-1, feat_width), mode="drop")
    )
    tile_scale = 1.0 / math.sqrt(F)
    partners = []
    for round_index in range(ROUNDS):
        partners.append(shifted(own_panel, "panel", round_index + 1))
    kinship = (
        jnp.concatenate(
            [
                lax.psum_scatter(
                    tile_of(own_panel, partner)[:, None, :], "feat", scatter_dimension=2, tiled=True
                )
                for partner in partners
            ],
            axis=1,
        )
        * tile_scale
    )
    return kinship


def hop(value, move):
    pairs = []
    for z in range(NZ):
        for y in range(NY):
            for x in range(NX):
                for c in range(NC):
                    to = move(z, y, x, c)
                    if to is not None:
                        tz, ty, tx, tc = to
                        pairs.append((((z * 2 + y) * 2 + x) * 2 + c, ((tz * 2 + ty) * 2 + tx) * 2 + tc))
    return lax.ppermute(value, BOTH, pairs)


def to_y(value):
    return hop(value, lambda z, y, x, c: (z, 1 - y, x, c))


def to_x(value):
    return hop(value, lambda z, y, x, c: (z, y, 1 - x, c))


def to_diagonal(value):
    return hop(value, lambda z, y, x, c: (z, 1 - y, 1 - x, c))


def to_core(value):
    return hop(value, lambda z, y, x, c: (z, y, x, 1 - c))


def z_ends(value):
    return hop(value, lambda z, y, x, c: (z ^ 1, y, x, c))


def z_middle(value):
    return hop(value, lambda z, y, x, c: (3 - z, y, x, c) if z in (1, 2) else (z, y, x, 1 - c))


def place():
    panel, feat = lax.axis_index("panel"), lax.axis_index("feat")
    return panel // NY, panel % NY, feat // NC, feat % NC


def call(kernel, out_shape, in_specs, out_specs, cost, scratch=(), limit=VMEM_LIMIT):
    return pl.pallas_call(
        kernel,
        name=kernel.func.__name__,
        out_shape=out_shape,
        in_specs=in_specs,
        out_specs=out_specs,
        scratch_shapes=scratch,
        compiler_params=pltpu.CompilerParams(vmem_limit_bytes=limit),
        cost_estimate=pl.CostEstimate(flops=cost[0], bytes_accessed=cost[1], transcendentals=0),
    )


IN_VMEM = pl.BlockSpec(memory_space=pltpu.VMEM)
IN_SMEM = pl.BlockSpec(memory_space=pltpu.SMEM)
ANYWHERE = pl.BlockSpec(memory_space=pl.ANY)
IN_HBM = pl.BlockSpec(memory_space=pltpu.HBM)


def bf16(*shape):
    return jax.ShapeDtypeStruct(shape, jnp.bfloat16)


def group_at(step):
    z, _, _, _ = place()
    group = jnp.int32(ORDER[0][step])
    for plane in range(1, NZ):
        group = jnp.where(z == plane, ORDER[plane][step], group)
    return group


def picks(slot, slots, step):
    group_rows = 2 * slots
    row = lax.broadcasted_iota(jnp.int32, (group_rows, slot.shape[1]), 0) + group_at(step) * group_rows
    return jnp.where(row == slot, 1.0, 0.0).astype(jnp.bfloat16)


def picked(pick, rows):
    return jnp.dot(pick, rows, preferred_element_type=jnp.float32).astype(jnp.bfloat16)


def columns_of_half(width, part):
    half = width // NY
    feat = lax.axis_index("feat")
    return (
        pl.ds(pl.multiple_of(part * half, half), half),
        pl.ds(pl.multiple_of(feat * width + part * half, half), half),
    )


def standard(dosage_ref, center_ref, weight_ref, part):
    columns, features = columns_of_half(dosage_ref.shape[1], part)
    rows = dosage_ref[:, columns].astype(jnp.float32)
    return ((rows - center_ref[:, features]) * weight_ref[:, features]).astype(jnp.bfloat16)


def first_kernel(
    slots,
    count_ref,
    assign_hbm,
    center_hbm,
    weight_hbm,
    dosage_hbm,
    slot_ref,
    counts_ref,
    rows_ref,
    away_ref,
    assign_ref,
    center_ref,
    weight_ref,
    dosage_ref,
    sems,
):
    capacity, half = dosage_ref.shape
    _, y, _, _ = place()
    panels = capacity // slots
    columns, features = columns_of_half(NY * half, 1 - y)
    copies = [
        pltpu.make_async_copy(assign_hbm, assign_ref, sems.at[0]),
        pltpu.make_async_copy(dosage_hbm.at[:, columns], dosage_ref, sems.at[1]),
        pltpu.make_async_copy(center_hbm.at[:, features], center_ref, sems.at[2]),
        pltpu.make_async_copy(weight_hbm.at[:, features], weight_ref, sems.at[3]),
    ]
    for copy in copies:
        copy.start()
    copies[0].wait()
    assign = assign_ref[...].reshape(1, capacity)
    lane = lax.broadcasted_iota(jnp.int32, (panels, capacity), 1)
    panel_id = lax.broadcasted_iota(jnp.int32, (panels, capacity), 0)
    live = lane < count_ref[0]
    member = (panel_id == assign) & live
    running = member.astype(jnp.int32)
    step = 1
    while step < capacity:
        running = running + jnp.where(lane >= step, pltpu.roll(running, step, 1), 0)
        step *= 2
    counts_ref[...] = jnp.broadcast_to(running[:, capacity - 1 :], counts_ref.shape)
    rank = jnp.sum(jnp.where(member, running - 1, 0), axis=0, keepdims=True)
    slot = jnp.where(live[:1], assign * slots + rank, -1)
    slot_ref[...] = slot
    for copy in copies[1:]:
        copy.wait()
    rows = dosage_ref[...].astype(jnp.float32)
    rows_ref[...] = ((rows - center_ref[...]) * weight_ref[...]).astype(jnp.bfloat16)
    at = 0
    for step in CHUNKS[0]:
        away_ref[pl.ds(at, 2 * slots), :] = picked(picks(slot, slots, step), rows_ref[...])
        at += 2 * slots


def rest_kernel(slots, slot_ref, rows_ref, center_ref, weight_ref, dosage_ref, own_ref, *away_refs):
    _, y, _, _ = place()
    group_rows = 2 * slots
    slot = slot_ref[...]
    pick = {}
    for chunk, away_ref in zip(CHUNKS[1:], away_refs):
        for k, step in enumerate(chunk):
            pick[step] = picks(slot, slots, step)
            away_ref[pl.ds(k * group_rows, group_rows), :] = picked(pick[step], rows_ref[...])
    stay = standard(dosage_ref, center_ref, weight_ref, y)
    for step in range(NZ):
        rows = pick[step] if step in pick else picks(slot, slots, step)
        own_ref[pl.ds(step * group_rows, group_rows), :] = picked(rows, stay)


def merge_kernel(slots, chunk, counts_ref, own_ref, other_ref, *out_refs):
    _, y, _, _ = place()
    row = lax.broadcasted_iota(jnp.int32, (PAIR_ROWS, slots), 0)
    slot = lax.broadcasted_iota(jnp.int32, (PAIR_ROWS, slots), 1)
    for at, (step, out_ref) in enumerate(zip(chunk, out_refs)):
        group = group_at(step)
        for k in range(2):
            n_own = counts_ref[group * 2 + k, 0]
            n_other = PAIR_ROWS - n_own
            own_at = jnp.where(y == 0, 0, n_other)
            other_at = jnp.where(y == 0, n_own, 0)
            pick_own = jnp.where((row == slot + own_at) & (slot < n_own), 1.0, 0.0).astype(jnp.bfloat16)
            pick_other = jnp.where((row == slot + other_at) & (slot < n_other), 1.0, 0.0).astype(jnp.bfloat16)
            merged = jnp.dot(
                pick_own, own_ref[pl.ds((step * 2 + k) * slots, slots), :], preferred_element_type=jnp.float32
            ) + jnp.dot(
                pick_other, other_ref[pl.ds((at * 2 + k) * slots, slots), :], preferred_element_type=jnp.float32
            )
            out_ref[pl.ds(k * PAIR_ROWS, PAIR_ROWS), :] = merged.astype(jnp.bfloat16)


def collect_kernel(names, whole, split, *refs):
    pieces = dict(zip(names, refs))
    send_ref, keep_ref, sems = refs[len(names) :]
    z, _, _, c = place()
    for zz in range(NZ):
        for cc in range(NC):

            @pl.when((z == zz) & (c == cc))
            def _(zz=zz, cc=cc):
                copies = []
                sent = kept = 0
                for r in whole + split:
                    g = (zz - r) % NZ
                    for s in range(NZ):
                        source = pieces["o%d" % ORDER[zz].index(g) if s == zz else FOUND[zz][s][g]]
                        if r in split and s % NC == cc:
                            copies.append((source, keep_ref.at[kept]))
                            kept += 1
                        else:
                            copies.append((source, send_ref.at[sent]))
                            sent += 1
                started = []
                for i, (source, target) in enumerate(copies):
                    copy = pltpu.make_async_copy(source, target, sems.at[i])
                    copy.start()
                    started.append(copy)
                for copy in started:
                    copy.wait()


def tile_kernel(tiles, n_kept, *refs):
    own_ref, own_far_ref = refs[:2]
    kept_refs = refs[2 : 2 + n_kept]
    far_refs = refs[2 + n_kept : 2 + 2 * n_kept]
    mine_ref, x_ref, y_ref, d_ref = refs[2 + 2 * n_kept :]
    _, y, x, c = place()
    depth = own_ref.shape[2]
    nt = (((1,), (1,)), ((), ()))

    def rows_of(ref, p):
        return ref[0:NZ, pl.ds(p * PAIR_ROWS, PAIR_ROWS), :].reshape(P_SIZE, depth)

    def columns_of(distance, q, part, near):
        rows = pl.ds(q * PAIR_ROWS, PAIR_ROWS)
        if distance == 0:
            return (own_ref if near else own_far_ref)[2 * part + c, rows, :]
        if near:
            return kept_refs[distance - 1][part, rows, :]
        ref = far_refs[distance - 1]
        first = ref.shape[0] - 2
        return ref[first + part, rows, :]

    for p in range(2):
        left, left_far = rows_of(own_ref, p), rows_of(own_far_ref, p)
        for part in range(2):
            near = jnp.concatenate([columns_of(d, q, part, True) for d, q in tiles[p]], axis=0)
            far = jnp.concatenate([columns_of(d, q, part, False) for d, q in tiles[p]], axis=0)
            total = lax.dot_general(left, near, nt, preferred_element_type=jnp.float32) + lax.dot_general(
                left_far, far, nt, preferred_element_type=jnp.float32
            )

            @pl.when((y == p) & (x == part))
            def _(total=total):
                mine_ref[...] = total

            @pl.when((y == p) & (x != part))
            def _(total=total):
                x_ref[...] = total.astype(jnp.bfloat16)

            @pl.when((y != p) & (x == part))
            def _(total=total):
                y_ref[...] = total.astype(jnp.bfloat16)

            @pl.when((y != p) & (x != part))
            def _(total=total):
                d_ref[...] = total.astype(jnp.bfloat16)


def plane_tiles(tiles, own, own_far, kept, far):
    columns = len(tiles[0]) * PAIR_ROWS
    part = bf16(P_SIZE, columns)
    mine, x_part, y_part, d_part = call(
        functools.partial(tile_kernel, tiles, len(kept)),
        (jax.ShapeDtypeStruct((P_SIZE, columns), jnp.float32), part, part, part),
        [IN_VMEM] * (2 + 2 * len(kept)),
        (IN_VMEM,) * 4,
        (2 * 4 * P_SIZE * columns * 2 * own.shape[2], 8 * 1024 * 1024),
    )(own, own_far, *kept, *far)
    return mine, to_y(y_part), to_diagonal(d_part), to_x(x_part)


def plane_shards(dosage, row_counts, assignment, center, weight):
    capacity, width = dosage.shape
    half = width // NY
    panels = NZ * NY
    slots = capacity // panels
    group_slots = 2 * slots
    group_rows = 2 * PAIR_ROWS

    center, weight = center.reshape(1, -1), weight.reshape(1, -1)
    chunk_rows = [len(chunk) * group_slots for chunk in CHUNKS]
    slot, counts, rows, away = call(
        functools.partial(first_kernel, slots),
        (
            jax.ShapeDtypeStruct((1, capacity), jnp.int32),
            jax.ShapeDtypeStruct((panels, 128), jnp.int32),
            bf16(capacity, half),
            bf16(chunk_rows[0], half),
        ),
        [IN_SMEM] + [ANYWHERE] * 4,
        (IN_VMEM,) * 4,
        (2 * chunk_rows[0] * capacity * half, 3 * capacity * width),
        (
            pltpu.VMEM((capacity,), jnp.int32),
            pltpu.VMEM((1, half), jnp.float32),
            pltpu.VMEM((1, half), jnp.float32),
            pltpu.VMEM((capacity, half), jnp.bfloat16),
            pltpu.SemaphoreType.DMA((4,)),
        ),
        FIRST_LIMIT,
    )(row_counts, assignment, center, weight, dosage)
    with jax.named_scope("y0"):
        came = [to_y(away)]
    own, *later = call(
        functools.partial(rest_kernel, slots),
        (bf16(capacity, half),) + tuple(bf16(n, half) for n in chunk_rows[1:]),
        [IN_VMEM] * 5,
        (IN_VMEM,) * len(CHUNKS),
        (2 * capacity * capacity * width, 3 * capacity * width),
    )(slot, rows, center, weight, dosage)
    for k, away in enumerate(later):
        with jax.named_scope("y%d" % (k + 1)):
            if k >= 1:
                away, _ = lax.optimization_barrier((away, came[k - 1]))
            came.append(to_y(away))
    pieces = {}
    z = lax.axis_index("panel") // NY

    sent = {z_ends: [], z_middle: []}

    def swap(move, name, value):
        before = sent[move]
        if len(before) >= WINDOW:
            value, _ = lax.optimization_barrier((value, pieces[before[-WINDOW]]))
        with jax.named_scope(name):
            pieces[name] = move(value)
        before.append(name)

    ends = functools.partial(swap, z_ends)
    middle = functools.partial(swap, z_middle)

    for chunk, other in zip(CHUNKS, came):
        if pieces:
            other, _ = lax.optimization_barrier((other, merged[-1]))
        if len(chunk) == 2:
            other, _, _ = lax.optimization_barrier((other, pieces["a0"], pieces["b0"]))
        merged = call(
            functools.partial(merge_kernel, slots, chunk),
            (bf16(group_rows, half),) * len(chunk),
            [IN_SMEM, IN_VMEM, IN_VMEM],
            (IN_VMEM,) * len(chunk),
            (2 * len(chunk) * group_rows * group_slots * half, 4 * group_rows * half * 2),
        )(counts, own, other)
        for step, piece in zip(chunk, merged):
            pieces["o%d" % step] = piece
            if step < NZ - 1:
                ends("a%d" % step, piece)
            middle("b%d" % step, piece)

    ends("a3", jnp.where((z == 0) | (z == 3), pieces["o3"], pieces["b0"]))
    for k in range(NZ):
        middle("c%d" % k, pieces["a%d" % k])
    for name, passed in (("d0", "b1"), ("d1", "b3"), ("e0", "c0"), ("e1", "c1"), ("e2", "c3")):
        ends(name, pieces[passed])

    def collect(whole, split):
        sent, kept = 4 * len(whole) + 2 * len(split), 2 * len(split)
        names = set()
        for z in range(NZ):
            for r in whole + split:
                g = (z - r) % NZ
                names.add("o%d" % ORDER[z].index(g))
                names.update(FOUND[z][s][g] for s in range(NZ) if s != z)
        names = sorted(names)
        return call(
            functools.partial(collect_kernel, names, whole, split),
            (bf16(sent, group_rows, half), bf16(kept, group_rows, half)),
            [ANYWHERE] * len(names),
            (ANYWHERE, ANYWHERE),
            (0, 4 * (sent + kept) * group_rows * half),
            (pltpu.SemaphoreType.DMA((sent + kept,)),),
        )(*[pieces[name] for name in names])

    sent1, kept1 = collect((0,), (1,))
    far1 = to_core(sent1)
    first = plane_tiles((((1, 1), (1, 0)), ((0, 0), (1, 1))), sent1, far1, (kept1,), (far1,))
    pieces["e2"], _ = lax.optimization_barrier((pieces["e2"], first[0]))
    sent2, kept2 = collect((), (2,))
    far2 = to_core(sent2)
    second = plane_tiles((((2, 1), (2, 0)), ((1, 0), (2, 1))), sent1, far1, (kept1, kept2), (far1, far2))

    def total(parts):
        mine, *others = parts
        for other in others:
            mine = mine + other.astype(jnp.float32)
        return mine.reshape(P_SIZE, 2, PAIR_ROWS)

    return jnp.concatenate([total(first), total(second)], axis=1) * (1.0 / math.sqrt(F))


def solution(mesh):
    in_specs = (P("panel", "feat"), P("panel"), P("panel"), P(), P())
    out_specs = P("panel", None, "feat")
    planes = mesh.shape["panel"] == NZ * NY and mesh.shape["feat"] == NX * NC
    shards = plane_shards if planes else general_shards
    return jax.shard_map(shards, mesh=mesh, in_specs=in_specs, out_specs=out_specs, check_vma=False)
```

```python
import functools
import math

import jax
import jax.numpy as jnp
from jax import lax
from jax.experimental import pallas as pl
from jax.experimental.pallas import tpu as pltpu
from jax.sharding import PartitionSpec as P

F = 4096
P_SIZE = 512
ROUNDS = 4
PAIR_ROWS = 128
NZ, NY, NX, NC = 4, 2, 2, 2
WINDOW = 9
VMEM_LIMIT = 40 * 1024 * 1024
FIRST_LIMIT = 62 * 1024 * 1024
BOTH = ("panel", "feat")
ORDER = ((2, 3, 0, 1), (3, 2, 0, 1), (3, 2, 1, 0), (0, 3, 1, 2))
LAST = "e2"
CHUNKS = ((0,), (1,), (2, 3))
FOUND = (
    {1: {3: "a0", 2: "a1", 0: "a2"}, 2: {3: "a3", 2: "d0", 0: "d1"}, 3: {0: "e0", 3: "e1", 2: "e2"}},
    {
        0: {2: "a0", 3: "a1", 0: "a2", 1: "a3"},
        2: {3: "b0", 2: "b1", 1: "b2", 0: "b3"},
        3: {0: "c0", 3: "c1", 1: "c2", 2: "c3"},
    },
    {
        3: {0: "a0", 3: "a1", 1: "a2", 2: "a3"},
        1: {3: "b0", 2: "b1", 0: "b2", 1: "b3"},
        0: {2: "c0", 3: "c1", 0: "c2", 1: "c3"},
    },
    {2: {3: "a0", 2: "a1", 1: "a2"}, 1: {3: "a3", 2: "d0", 1: "d1"}, 0: {2: "e0", 3: "e1", 1: "e2"}},
)


def shifted(value, axis, steps):
    count = lax.axis_size(axis)
    pairs = [(source, (source + steps) % count) for source in range(count)]
    return lax.ppermute(value, axis, pairs)


def tile_of(left_rows, partner):
    return lax.dot_general(
        left_rows, partner, (((1,), (1,)), ((), ())), preferred_element_type=jnp.float32
    )


def general_shards(dosage, row_counts, assignment, center, weight):
    panel_total = lax.axis_size("panel")
    feat_index = lax.axis_index("feat")
    capacity = dosage.shape[0]
    feat_width = dosage.shape[1]
    send_rows = capacity // panel_total
    feat_start = feat_index * feat_width
    center_part = lax.dynamic_slice_in_dim(center, feat_start, feat_width)
    weight_part = lax.dynamic_slice_in_dim(weight, feat_start, feat_width)
    standard = ((dosage.astype(jnp.float32) - center_part) * weight_part).astype(jnp.bfloat16)
    slot_ids = jnp.arange(capacity, dtype=jnp.int32)
    live_rows = slot_ids < row_counts[0]
    targets = jnp.arange(panel_total, dtype=jnp.int32)
    onehot = ((assignment[:, None] == targets[None, :]) & live_rows[:, None]).astype(jnp.int32)
    earlier = jnp.sum((jnp.cumsum(onehot, axis=0) - onehot) * onehot, axis=1)
    slot_index = jnp.where(live_rows, assignment * send_rows + earlier, panel_total * send_rows)
    outgoing = (
        jnp.zeros((panel_total * send_rows, feat_width), jnp.bfloat16)
        .at[slot_index]
        .set(standard, mode="drop")
    )
    outgoing = outgoing.reshape(panel_total, send_rows, feat_width)
    sent_counts = jnp.sum(onehot, axis=0).reshape(panel_total, 1)
    incoming, arrived = (
        lax.all_to_all(outgoing, "panel", split_axis=0, concat_axis=0, tiled=True),
        lax.all_to_all(sent_counts, "panel", split_axis=0, concat_axis=0, tiled=True),
    )
    arrived_rows = arrived[:, 0]
    offsets = jnp.cumsum(arrived_rows) - arrived_rows
    within = jnp.arange(send_rows, dtype=jnp.int32)
    positions = jnp.where(
        within[None, :] < arrived_rows[:, None], offsets[:, None] + within[None, :], P_SIZE
    )
    own_panel = (
        jnp.zeros((P_SIZE, feat_width), jnp.bfloat16)
        .at[positions.reshape(-1)]
        .set(incoming.reshape(-1, feat_width), mode="drop")
    )
    tile_scale = 1.0 / math.sqrt(F)
    partners = []
    for round_index in range(ROUNDS):
        partners.append(shifted(own_panel, "panel", round_index + 1))
    kinship = (
        jnp.concatenate(
            [
                lax.psum_scatter(
                    tile_of(own_panel, partner)[:, None, :], "feat", scatter_dimension=2, tiled=True
                )
                for partner in partners
            ],
            axis=1,
        )
        * tile_scale
    )
    return kinship


def hop(value, move):
    pairs = []
    for z in range(NZ):
        for y in range(NY):
            for x in range(NX):
                for c in range(NC):
                    to = move(z, y, x, c)
                    if to is not None:
                        tz, ty, tx, tc = to
                        pairs.append((((z * 2 + y) * 2 + x) * 2 + c, ((tz * 2 + ty) * 2 + tx) * 2 + tc))
    return lax.ppermute(value, BOTH, pairs)


def to_y(value):
    return hop(value, lambda z, y, x, c: (z, 1 - y, x, c))


def to_x(value):
    return hop(value, lambda z, y, x, c: (z, y, 1 - x, c))


def to_diagonal(value):
    return hop(value, lambda z, y, x, c: (z, 1 - y, 1 - x, c))


def to_core(value):
    return hop(value, lambda z, y, x, c: (z, y, x, 1 - c))


def z_ends(value):
    return hop(value, lambda z, y, x, c: (z ^ 1, y, x, c))


def z_last(value, far):
    def move(z, y, x, c):
        to = 1 - c if far else c
        receiver = 1 if z in (0, 1) else 0
        if (c if z in (0, 3) else to) == receiver:
            return z ^ 1, y, x, to
        return z, y, 1 - x, c

    return hop(value, move)


def z_middle(value):
    return hop(value, lambda z, y, x, c: (3 - z, y, x, c) if z in (1, 2) else (z, y, x, 1 - c))


def place():
    panel, feat = lax.axis_index("panel"), lax.axis_index("feat")
    return panel // NY, panel % NY, feat // NC, feat % NC


def call(kernel, out_shape, in_specs, out_specs, cost, scratch=(), limit=VMEM_LIMIT):
    return pl.pallas_call(
        kernel,
        name=kernel.func.__name__,
        out_shape=out_shape,
        in_specs=in_specs,
        out_specs=out_specs,
        scratch_shapes=scratch,
        compiler_params=pltpu.CompilerParams(vmem_limit_bytes=limit),
        cost_estimate=pl.CostEstimate(flops=cost[0], bytes_accessed=cost[1], transcendentals=0),
    )


IN_VMEM = pl.BlockSpec(memory_space=pltpu.VMEM)
IN_SMEM = pl.BlockSpec(memory_space=pltpu.SMEM)
ANYWHERE = pl.BlockSpec(memory_space=pl.ANY)
IN_HBM = pl.BlockSpec(memory_space=pltpu.HBM)


def bf16(*shape):
    return jax.ShapeDtypeStruct(shape, jnp.bfloat16)


def group_at(step):
    z, _, _, _ = place()
    group = jnp.int32(ORDER[0][step])
    for plane in range(1, NZ):
        group = jnp.where(z == plane, ORDER[plane][step], group)
    return group


def picks(slot, slots, step):
    group_rows = 2 * slots
    row = lax.broadcasted_iota(jnp.int32, (group_rows, slot.shape[1]), 0) + group_at(step) * group_rows
    return jnp.where(row == slot, 1.0, 0.0).astype(jnp.bfloat16)


def picked(pick, rows):
    return jnp.dot(pick, rows, preferred_element_type=jnp.float32).astype(jnp.bfloat16)


def columns_of_half(width, part):
    half = width // NY
    feat = lax.axis_index("feat")
    return (
        pl.ds(pl.multiple_of(part * half, half), half),
        pl.ds(pl.multiple_of(feat * width + part * half, half), half),
    )


def standard(dosage_ref, center_ref, weight_ref, part):
    columns, features = columns_of_half(dosage_ref.shape[1], part)
    rows = dosage_ref[:, columns].astype(jnp.float32)
    return ((rows - center_ref[:, features]) * weight_ref[:, features]).astype(jnp.bfloat16)


def first_kernel(
    slots,
    count_ref,
    assign_hbm,
    center_hbm,
    weight_hbm,
    dosage_hbm,
    slot_ref,
    counts_ref,
    rows_ref,
    away_ref,
    assign_ref,
    center_ref,
    weight_ref,
    dosage_ref,
    sems,
):
    capacity, half = dosage_ref.shape
    _, y, _, _ = place()
    panels = capacity // slots
    columns, features = columns_of_half(NY * half, 1 - y)
    copies = [
        pltpu.make_async_copy(assign_hbm, assign_ref, sems.at[0]),
        pltpu.make_async_copy(dosage_hbm.at[:, columns], dosage_ref, sems.at[1]),
        pltpu.make_async_copy(center_hbm.at[:, features], center_ref, sems.at[2]),
        pltpu.make_async_copy(weight_hbm.at[:, features], weight_ref, sems.at[3]),
    ]
    for copy in copies:
        copy.start()
    copies[0].wait()
    assign = assign_ref[...].reshape(1, capacity)
    lane = lax.broadcasted_iota(jnp.int32, (panels, capacity), 1)
    panel_id = lax.broadcasted_iota(jnp.int32, (panels, capacity), 0)
    live = lane < count_ref[0]
    member = (panel_id == assign) & live
    running = member.astype(jnp.int32)
    step = 1
    while step < capacity:
        running = running + jnp.where(lane >= step, pltpu.roll(running, step, 1), 0)
        step *= 2
    counts_ref[...] = jnp.broadcast_to(running[:, capacity - 1 :], counts_ref.shape)
    rank = jnp.sum(jnp.where(member, running - 1, 0), axis=0, keepdims=True)
    slot = jnp.where(live[:1], assign * slots + rank, -1)
    slot_ref[...] = slot
    for copy in copies[1:]:
        copy.wait()
    rows = dosage_ref[...].astype(jnp.float32)
    rows_ref[...] = ((rows - center_ref[...]) * weight_ref[...]).astype(jnp.bfloat16)
    at = 0
    for step in CHUNKS[0]:
        away_ref[pl.ds(at, 2 * slots), :] = picked(picks(slot, slots, step), rows_ref[...])
        at += 2 * slots


def rest_kernel(slots, slot_ref, rows_ref, center_ref, weight_ref, dosage_ref, own_ref, *away_refs):
    _, y, _, _ = place()
    group_rows = 2 * slots
    slot = slot_ref[...]
    pick = {}
    for chunk, away_ref in zip(CHUNKS[1:], away_refs):
        for k, step in enumerate(chunk):
            pick[step] = picks(slot, slots, step)
            away_ref[pl.ds(k * group_rows, group_rows), :] = picked(pick[step], rows_ref[...])
    stay = standard(dosage_ref, center_ref, weight_ref, y)
    for step in range(NZ):
        rows = pick[step] if step in pick else picks(slot, slots, step)
        own_ref[pl.ds(step * group_rows, group_rows), :] = picked(rows, stay)


def merge_kernel(slots, chunk, counts_ref, own_ref, other_ref, *out_refs):
    _, y, _, _ = place()
    row = lax.broadcasted_iota(jnp.int32, (PAIR_ROWS, slots), 0)
    slot = lax.broadcasted_iota(jnp.int32, (PAIR_ROWS, slots), 1)
    for at, (step, out_ref) in enumerate(zip(chunk, out_refs)):
        group = group_at(step)
        for k in range(2):
            n_own = counts_ref[group * 2 + k, 0]
            n_other = PAIR_ROWS - n_own
            own_at = jnp.where(y == 0, 0, n_other)
            other_at = jnp.where(y == 0, n_own, 0)
            pick_own = jnp.where((row == slot + own_at) & (slot < n_own), 1.0, 0.0).astype(jnp.bfloat16)
            pick_other = jnp.where((row == slot + other_at) & (slot < n_other), 1.0, 0.0).astype(jnp.bfloat16)
            merged = jnp.dot(
                pick_own, own_ref[pl.ds((step * 2 + k) * slots, slots), :], preferred_element_type=jnp.float32
            ) + jnp.dot(
                pick_other, other_ref[pl.ds((at * 2 + k) * slots, slots), :], preferred_element_type=jnp.float32
            )
            out_ref[pl.ds(k * PAIR_ROWS, PAIR_ROWS), :] = merged.astype(jnp.bfloat16)


def collect_kernel(names, whole, split, *refs):
    pieces = dict(zip(names, refs))
    send_ref, keep_ref, sems = refs[len(names) :]
    z, _, _, c = place()
    for zz in range(NZ):
        for cc in range(NC):

            @pl.when((z == zz) & (c == cc))
            def _(zz=zz, cc=cc):
                copies = []
                sent = kept = 0
                for r in whole + split:
                    g = (zz - r) % NZ
                    for s in range(NZ):
                        name = "o%d" % ORDER[zz].index(g) if s == zz else FOUND[zz][s][g]
                        if r in split and s % NC == cc:
                            target = keep_ref.at[kept]
                            kept += 1
                        else:
                            target = send_ref.at[sent]
                            sent += 1
                        if name != LAST:
                            copies.append((pieces[name], target))
                started = []
                for i, (source, target) in enumerate(copies):
                    copy = pltpu.make_async_copy(source, target, sems.at[i])
                    copy.start()
                    started.append(copy)
                for copy in started:
                    copy.wait()


def tile_kernel(tiles, sent_ref, far_ref, kept_ref, *refs):
    mine_ref, x_ref, y_ref, d_ref = refs[2:6] if len(refs) > 4 else refs
    z, y, x, c = place()
    depth = sent_ref.shape[2]
    nt = (((1,), (1,)), ((), ()))
    if len(refs) > 4:
        last_ref, last_far_ref = refs[:2]
        near2_ref, far2_ref = refs[6:]
        for part in range(2):
            here = ((z == 0) & (c == 1)) if part == 1 else ((z == 3) & (c == 0))

            @pl.when(here)
            def _(part=part):
                near2_ref[part] = last_ref[...]
                far2_ref[part] = last_far_ref[...]

            @pl.when(jnp.logical_not(here))
            def _(part=part):
                near2_ref[part] = kept_ref[2 + part]
                far2_ref[part] = far_ref[NZ + 2 + part]

    def rows_of(ref, p):
        return ref[0:NZ, pl.ds(p * PAIR_ROWS, PAIR_ROWS), :].reshape(P_SIZE, depth)

    def columns_of(distance, q, part, near):
        rows = pl.ds(q * PAIR_ROWS, PAIR_ROWS)
        if distance == 0:
            return (sent_ref if near else far_ref)[2 * part + c, rows, :]
        if distance == 1:
            return kept_ref[part, rows, :] if near else far_ref[NZ + part, rows, :]
        return (near2_ref if near else far2_ref)[part, rows, :]

    for p in range(2):
        for mine in (True, False):

            @pl.when((y == p) if mine else (y != p))
            def _(p=p, mine=mine):
                left, left_far = rows_of(sent_ref, p), rows_of(far_ref, p)
                for part, out_ref in ((x, mine_ref if mine else y_ref), (1 - x, x_ref if mine else d_ref)):
                    near = jnp.concatenate([columns_of(d, q, part, True) for d, q in tiles[p]], axis=0)
                    far = jnp.concatenate([columns_of(d, q, part, False) for d, q in tiles[p]], axis=0)
                    total = lax.dot_general(left, near, nt, preferred_element_type=jnp.float32) + lax.dot_general(
                        left_far, far, nt, preferred_element_type=jnp.float32
                    )
                    out_ref[...] = total.astype(out_ref.dtype)


def plane_tiles(tiles, sent, far, kept, *last):
    columns = len(tiles[0]) * PAIR_ROWS
    part = bf16(P_SIZE, columns)
    room = (2, *sent.shape[1:])
    mine, x_part, y_part, d_part = call(
        functools.partial(tile_kernel, tiles),
        (jax.ShapeDtypeStruct((P_SIZE, columns), jnp.float32), part, part, part),
        [IN_VMEM] * (3 + len(last)),
        (IN_VMEM,) * 4,
        (2 * 4 * P_SIZE * columns * 2 * sent.shape[2], 8 * 1024 * 1024),
        (pltpu.VMEM(room, jnp.bfloat16),) * 2 if last else (),
    )(sent, far, kept, *last)
    return mine, y_part, d_part, x_part


def plane_shards(dosage, row_counts, assignment, center, weight):
    capacity, width = dosage.shape
    half = width // NY
    panels = NZ * NY
    slots = capacity // panels
    group_slots = 2 * slots
    group_rows = 2 * PAIR_ROWS

    center, weight = center.reshape(1, -1), weight.reshape(1, -1)
    chunk_rows = [len(chunk) * group_slots for chunk in CHUNKS]
    slot, counts, rows, away = call(
        functools.partial(first_kernel, slots),
        (
            jax.ShapeDtypeStruct((1, capacity), jnp.int32),
            jax.ShapeDtypeStruct((panels, 128), jnp.int32),
            bf16(capacity, half),
            bf16(chunk_rows[0], half),
        ),
        [IN_SMEM] + [ANYWHERE] * 4,
        (IN_VMEM,) * 4,
        (2 * chunk_rows[0] * capacity * half, 3 * capacity * width),
        (
            pltpu.VMEM((capacity,), jnp.int32),
            pltpu.VMEM((1, half), jnp.float32),
            pltpu.VMEM((1, half), jnp.float32),
            pltpu.VMEM((capacity, half), jnp.bfloat16),
            pltpu.SemaphoreType.DMA((4,)),
        ),
        FIRST_LIMIT,
    )(row_counts, assignment, center, weight, dosage)
    with jax.named_scope("y0"):
        came = [to_y(away)]
    own, *later = call(
        functools.partial(rest_kernel, slots),
        (bf16(capacity, half),) + tuple(bf16(n, half) for n in chunk_rows[1:]),
        [IN_VMEM] * 5,
        (IN_VMEM,) * len(CHUNKS),
        (2 * capacity * capacity * width, 3 * capacity * width),
    )(slot, rows, center, weight, dosage)
    for k, away in enumerate(later):
        with jax.named_scope("y%d" % (k + 1)):
            if k >= 1:
                away, _ = lax.optimization_barrier((away, came[k - 1]))
            came.append(to_y(away))
    pieces = {}
    z = lax.axis_index("panel") // NY

    queues = {z_ends: [], z_middle: []}

    def swap(move, name, value):
        before = queues[move]
        if len(before) >= WINDOW:
            value, _ = lax.optimization_barrier((value, pieces[before[-WINDOW]]))
        with jax.named_scope(name):
            pieces[name] = move(value)
        before.append(name)

    ends = functools.partial(swap, z_ends)
    middle = functools.partial(swap, z_middle)

    for chunk, other in zip(CHUNKS, came):
        if pieces:
            other, _ = lax.optimization_barrier((other, merged[-1]))
        if len(chunk) == 2:
            other, _, _ = lax.optimization_barrier((other, pieces["a0"], pieces["b0"]))
        merged = call(
            functools.partial(merge_kernel, slots, chunk),
            (bf16(group_rows, half),) * len(chunk),
            [IN_SMEM, IN_VMEM, IN_VMEM],
            (IN_VMEM,) * len(chunk),
            (2 * len(chunk) * group_rows * group_slots * half, 4 * group_rows * half * 2),
        )(counts, own, other)
        for step, piece in zip(chunk, merged):
            pieces["o%d" % step] = piece
            if step < NZ - 1:
                ends("a%d" % step, piece)
            middle("b%d" % step, piece)

    ends("a3", jnp.where((z == 0) | (z == 3), pieces["o3"], pieces["b0"]))
    pieces["a1"], pieces["b1"], _, _ = lax.optimization_barrier((pieces["a1"], pieces["b1"], pieces["a0"], pieces["b0"]))
    for k in range(NZ):
        middle("c%d" % k, pieces["a%d" % k])
    for name, passed in (("d0", "b1"), ("d1", "b3"), ("e0", "c0"), ("e1", "c1")):
        ends(name, pieces[passed])
    with jax.named_scope("last"):
        last = z_last(pieces["c3"], False), z_last(pieces["c3"], True)

    names = set()
    for plane in range(NZ):
        for r in range(3):
            g = (plane - r) % NZ
            names.add("o%d" % ORDER[plane].index(g))
            names.update(FOUND[plane][s][g] for s in range(NZ) if s != plane)
    names = sorted(names - {LAST})
    sent, kept = call(
        functools.partial(collect_kernel, names, (0,), (1, 2)),
        (bf16(2 * NZ, group_rows, half), bf16(NZ, group_rows, half)),
        [ANYWHERE] * len(names),
        (ANYWHERE, ANYWHERE),
        (0, 4 * 3 * NZ * group_rows * half),
        (pltpu.SemaphoreType.DMA((3 * NZ,)),),
    )(*[pieces[name] for name in names])
    far = to_core(sent)
    first = plane_tiles((((1, 1), (1, 0)), ((0, 0), (1, 1))), sent, far, kept)
    second = plane_tiles((((2, 1), (2, 0)), ((1, 0), (2, 1))), sent, far, kept, *last)

    def exchanged(mine, y_part, d_part, x_part):
        return mine, to_y(y_part), to_diagonal(d_part), to_x(x_part)

    first = exchanged(*first)
    x_part, _ = lax.optimization_barrier((second[3], first[3]))
    second = exchanged(*second[:3], x_part)

    def total(parts):
        mine, *others = parts
        for other in others:
            mine = mine + other.astype(jnp.float32)
        return mine.reshape(P_SIZE, 2, PAIR_ROWS)

    return jnp.concatenate([total(first), total(second)], axis=1) * (1.0 / math.sqrt(F))


def solution(mesh):
    in_specs = (P("panel", "feat"), P("panel"), P("panel"), P(), P())
    out_specs = P("panel", None, "feat")
    planes = mesh.shape["panel"] == NZ * NY and mesh.shape["feat"] == NX * NC
    shards = plane_shards if planes else general_shards
    return jax.shard_map(shards, mesh=mesh, in_specs=in_specs, out_specs=out_specs, check_vma=False)
```

```python
import functools
import math

import jax
import jax.numpy as jnp
from jax import lax
from jax.experimental import pallas as pl
from jax.experimental.pallas import tpu as pltpu
from jax.sharding import PartitionSpec as P

F = 4096
P_SIZE = 512
ROUNDS = 4
PAIR_ROWS = 128
NZ, NY, NX, NC = 4, 2, 2, 2
AFTER = {"a2": ("e1",), "c0": ("d0",), "c1": ("a2",), "d1": ("a3",), "first_d": ("b2", "y2", "e1",), "m2": ("a0", "b0",), "p_b0": ("a0",), "pp2": ("e1",), "second_d": ("pp2",), "second_x": ("l0",), "y2": ("y0",)}
VMEM_LIMIT = 40 * 1024 * 1024
FIRST_LIMIT = 62 * 1024 * 1024
BOTH = ("panel", "feat")
ORDER = ((2, 3, 0, 1), (3, 2, 0, 1), (3, 2, 1, 0), (0, 3, 1, 2))
LAST = "e2"
CHUNKS = ((0,), (1,), (2, 3))
FOUND = (
    {1: {3: "a0", 2: "a1", 0: "a2"}, 2: {3: "a3", 2: "d0", 0: "d1"}, 3: {0: "e0", 3: "e1", 2: "e2"}},
    {
        0: {2: "a0", 3: "a1", 0: "a2", 1: "a3"},
        2: {3: "b0", 2: "b1", 1: "b2", 0: "b3"},
        3: {0: "c0", 3: "c1", 1: "c2", 2: "c3"},
    },
    {
        3: {0: "a0", 3: "a1", 1: "a2", 2: "a3"},
        1: {3: "b0", 2: "b1", 0: "b2", 1: "b3"},
        0: {2: "c0", 3: "c1", 0: "c2", 1: "c3"},
    },
    {2: {3: "a0", 2: "a1", 1: "a2"}, 1: {3: "a3", 2: "d0", 1: "d1"}, 0: {2: "e0", 3: "e1", 1: "e2"}},
)


def shifted(value, axis, steps):
    count = lax.axis_size(axis)
    pairs = [(source, (source + steps) % count) for source in range(count)]
    return lax.ppermute(value, axis, pairs)


def tile_of(left_rows, partner):
    return lax.dot_general(
        left_rows, partner, (((1,), (1,)), ((), ())), preferred_element_type=jnp.float32
    )


def general_shards(dosage, row_counts, assignment, center, weight):
    panel_total = lax.axis_size("panel")
    feat_index = lax.axis_index("feat")
    capacity = dosage.shape[0]
    feat_width = dosage.shape[1]
    send_rows = capacity // panel_total
    feat_start = feat_index * feat_width
    center_part = lax.dynamic_slice_in_dim(center, feat_start, feat_width)
    weight_part = lax.dynamic_slice_in_dim(weight, feat_start, feat_width)
    standard = ((dosage.astype(jnp.float32) - center_part) * weight_part).astype(jnp.bfloat16)
    slot_ids = jnp.arange(capacity, dtype=jnp.int32)
    live_rows = slot_ids < row_counts[0]
    targets = jnp.arange(panel_total, dtype=jnp.int32)
    onehot = ((assignment[:, None] == targets[None, :]) & live_rows[:, None]).astype(jnp.int32)
    earlier = jnp.sum((jnp.cumsum(onehot, axis=0) - onehot) * onehot, axis=1)
    slot_index = jnp.where(live_rows, assignment * send_rows + earlier, panel_total * send_rows)
    outgoing = (
        jnp.zeros((panel_total * send_rows, feat_width), jnp.bfloat16)
        .at[slot_index]
        .set(standard, mode="drop")
    )
    outgoing = outgoing.reshape(panel_total, send_rows, feat_width)
    sent_counts = jnp.sum(onehot, axis=0).reshape(panel_total, 1)
    incoming, arrived = (
        lax.all_to_all(outgoing, "panel", split_axis=0, concat_axis=0, tiled=True),
        lax.all_to_all(sent_counts, "panel", split_axis=0, concat_axis=0, tiled=True),
    )
    arrived_rows = arrived[:, 0]
    offsets = jnp.cumsum(arrived_rows) - arrived_rows
    within = jnp.arange(send_rows, dtype=jnp.int32)
    positions = jnp.where(
        within[None, :] < arrived_rows[:, None], offsets[:, None] + within[None, :], P_SIZE
    )
    own_panel = (
        jnp.zeros((P_SIZE, feat_width), jnp.bfloat16)
        .at[positions.reshape(-1)]
        .set(incoming.reshape(-1, feat_width), mode="drop")
    )
    tile_scale = 1.0 / math.sqrt(F)
    partners = []
    for round_index in range(ROUNDS):
        partners.append(shifted(own_panel, "panel", round_index + 1))
    kinship = (
        jnp.concatenate(
            [
                lax.psum_scatter(
                    tile_of(own_panel, partner)[:, None, :], "feat", scatter_dimension=2, tiled=True
                )
                for partner in partners
            ],
            axis=1,
        )
        * tile_scale
    )
    return kinship


def hop(value, move):
    pairs = []
    for z in range(NZ):
        for y in range(NY):
            for x in range(NX):
                for c in range(NC):
                    to = move(z, y, x, c)
                    if to is not None:
                        tz, ty, tx, tc = to
                        pairs.append((((z * 2 + y) * 2 + x) * 2 + c, ((tz * 2 + ty) * 2 + tx) * 2 + tc))
    return lax.ppermute(value, BOTH, pairs)


def to_y(value):
    return hop(value, lambda z, y, x, c: (z, 1 - y, x, c))


def to_x(value):
    return hop(value, lambda z, y, x, c: (z, y, 1 - x, c))


def to_diagonal(value):
    return hop(value, lambda z, y, x, c: (z, 1 - y, 1 - x, c))


def to_core(value):
    return hop(value, lambda z, y, x, c: (z, y, x, 1 - c))


def z_ends(value):
    return hop(value, lambda z, y, x, c: (z ^ 1, y, x, c))


def z_last(value, far):
    def move(z, y, x, c):
        to = 1 - c if far else c
        receiver = 1 if z in (0, 1) else 0
        if (c if z in (0, 3) else to) == receiver:
            return z ^ 1, y, x, to
        return z, y, 1 - x, c

    return hop(value, move)


def z_middle(value):
    return hop(value, lambda z, y, x, c: (3 - z, y, x, c) if z in (1, 2) else (z, y, x, 1 - c))


def place():
    panel, feat = lax.axis_index("panel"), lax.axis_index("feat")
    return panel // NY, panel % NY, feat // NC, feat % NC


def call(kernel, out_shape, in_specs, out_specs, cost, scratch=(), limit=VMEM_LIMIT):
    return pl.pallas_call(
        kernel,
        name=kernel.func.__name__,
        out_shape=out_shape,
        in_specs=in_specs,
        out_specs=out_specs,
        scratch_shapes=scratch,
        compiler_params=pltpu.CompilerParams(vmem_limit_bytes=limit),
        cost_estimate=pl.CostEstimate(flops=cost[0], bytes_accessed=cost[1], transcendentals=0),
    )


IN_VMEM = pl.BlockSpec(memory_space=pltpu.VMEM)
IN_SMEM = pl.BlockSpec(memory_space=pltpu.SMEM)
ANYWHERE = pl.BlockSpec(memory_space=pl.ANY)
IN_HBM = pl.BlockSpec(memory_space=pltpu.HBM)


def bf16(*shape):
    return jax.ShapeDtypeStruct(shape, jnp.bfloat16)


def group_at(step):
    z, _, _, _ = place()
    group = jnp.int32(ORDER[0][step])
    for plane in range(1, NZ):
        group = jnp.where(z == plane, ORDER[plane][step], group)
    return group


def picks(slot, slots, step):
    group_rows = 2 * slots
    row = lax.broadcasted_iota(jnp.int32, (group_rows, slot.shape[1]), 0) + group_at(step) * group_rows
    return jnp.where(row == slot, 1.0, 0.0).astype(jnp.bfloat16)


def picked(pick, rows):
    return jnp.dot(pick, rows, preferred_element_type=jnp.float32).astype(jnp.bfloat16)


def columns_of_half(width, part):
    half = width // NY
    feat = lax.axis_index("feat")
    return (
        pl.ds(pl.multiple_of(part * half, half), half),
        pl.ds(pl.multiple_of(feat * width + part * half, half), half),
    )


def standard(dosage_ref, center_ref, weight_ref, part):
    columns, features = columns_of_half(dosage_ref.shape[1], part)
    rows = dosage_ref[:, columns].astype(jnp.float32)
    return ((rows - center_ref[:, features]) * weight_ref[:, features]).astype(jnp.bfloat16)


def first_kernel(
    slots,
    count_ref,
    assign_hbm,
    center_hbm,
    weight_hbm,
    dosage_hbm,
    slot_ref,
    counts_ref,
    rows_ref,
    away_ref,
    assign_ref,
    center_ref,
    weight_ref,
    dosage_ref,
    sems,
):
    capacity, half = dosage_ref.shape
    _, y, _, _ = place()
    panels = capacity // slots
    columns, features = columns_of_half(NY * half, 1 - y)
    copies = [
        pltpu.make_async_copy(assign_hbm, assign_ref, sems.at[0]),
        pltpu.make_async_copy(dosage_hbm.at[:, columns], dosage_ref, sems.at[1]),
        pltpu.make_async_copy(center_hbm.at[:, features], center_ref, sems.at[2]),
        pltpu.make_async_copy(weight_hbm.at[:, features], weight_ref, sems.at[3]),
    ]
    for copy in copies:
        copy.start()
    copies[0].wait()
    assign = assign_ref[...].reshape(1, capacity)
    lane = lax.broadcasted_iota(jnp.int32, (panels, capacity), 1)
    panel_id = lax.broadcasted_iota(jnp.int32, (panels, capacity), 0)
    live = lane < count_ref[0]
    member = (panel_id == assign) & live
    running = member.astype(jnp.int32)
    step = 1
    while step < capacity:
        running = running + jnp.where(lane >= step, pltpu.roll(running, step, 1), 0)
        step *= 2
    counts_ref[...] = jnp.broadcast_to(running[:, capacity - 1 :], counts_ref.shape)
    rank = jnp.sum(jnp.where(member, running - 1, 0), axis=0, keepdims=True)
    slot = jnp.where(live[:1], assign * slots + rank, -1)
    slot_ref[...] = slot
    for copy in copies[1:]:
        copy.wait()
    rows = dosage_ref[...].astype(jnp.float32)
    rows_ref[...] = ((rows - center_ref[...]) * weight_ref[...]).astype(jnp.bfloat16)
    at = 0
    for step in CHUNKS[0]:
        away_ref[pl.ds(at, 2 * slots), :] = picked(picks(slot, slots, step), rows_ref[...])
        at += 2 * slots


def rest_kernel(slots, slot_ref, rows_ref, center_ref, weight_ref, dosage_ref, own_ref, *away_refs):
    _, y, _, _ = place()
    group_rows = 2 * slots
    slot = slot_ref[...]
    pick = {}
    for chunk, away_ref in zip(CHUNKS[1:], away_refs):
        for k, step in enumerate(chunk):
            pick[step] = picks(slot, slots, step)
            away_ref[pl.ds(k * group_rows, group_rows), :] = picked(pick[step], rows_ref[...])
    stay = standard(dosage_ref, center_ref, weight_ref, y)
    for step in range(NZ):
        rows = pick[step] if step in pick else picks(slot, slots, step)
        own_ref[pl.ds(step * group_rows, group_rows), :] = picked(rows, stay)


def merge_kernel(slots, chunk, counts_ref, own_ref, other_ref, *out_refs):
    _, y, _, _ = place()
    row = lax.broadcasted_iota(jnp.int32, (PAIR_ROWS, slots), 0)
    slot = lax.broadcasted_iota(jnp.int32, (PAIR_ROWS, slots), 1)
    for at, (step, out_ref) in enumerate(zip(chunk, out_refs)):
        group = group_at(step)
        for k in range(2):
            n_own = counts_ref[group * 2 + k, 0]
            n_other = PAIR_ROWS - n_own
            own_at = jnp.where(y == 0, 0, n_other)
            other_at = jnp.where(y == 0, n_own, 0)
            pick_own = jnp.where((row == slot + own_at) & (slot < n_own), 1.0, 0.0).astype(jnp.bfloat16)
            pick_other = jnp.where((row == slot + other_at) & (slot < n_other), 1.0, 0.0).astype(jnp.bfloat16)
            merged = jnp.dot(
                pick_own, own_ref[pl.ds((step * 2 + k) * slots, slots), :], preferred_element_type=jnp.float32
            ) + jnp.dot(
                pick_other, other_ref[pl.ds((at * 2 + k) * slots, slots), :], preferred_element_type=jnp.float32
            )
            out_ref[pl.ds(k * PAIR_ROWS, PAIR_ROWS), :] = merged.astype(jnp.bfloat16)


def collect_kernel(names, whole, split, *refs):
    pieces = dict(zip(names, refs))
    send_ref, later_ref, keep_ref, sems = refs[len(names) :]
    z, _, _, c = place()
    for zz in range(NZ):
        for cc in range(NC):

            @pl.when((z == zz) & (c == cc))
            def _(zz=zz, cc=cc):
                copies = []
                sent = kept = 0
                for r in whole + split:
                    g = (zz - r) % NZ
                    for s in range(NZ):
                        name = "o%d" % ORDER[zz].index(g) if s == zz else FOUND[zz][s][g]
                        if r in split and s % NC == cc:
                            target = keep_ref.at[kept]
                            kept += 1
                        else:
                            room = send_ref.shape[0]
                            target = send_ref.at[sent] if sent < room else later_ref.at[sent - room]
                            sent += 1
                        if name != LAST:
                            copies.append((pieces[name], target))
                started = []
                for i, (source, target) in enumerate(copies):
                    copy = pltpu.make_async_copy(source, target, sems.at[i])
                    copy.start()
                    started.append(copy)
                for copy in started:
                    copy.wait()


def tile_kernel(tiles, mine, sent_ref, far_ref, kept_ref, *refs):
    *lasts, here_ref, there_ref = refs[:2] if len(refs) == 2 else refs[:5]
    z, y, x, c = place()
    depth = sent_ref.shape[2]
    nt = (((1,), (1,)), ((), ()))
    if lasts:
        last_ref, last_far_ref, far_later_ref = lasts
        near2_ref, far2_ref = refs[5:]
        for part in range(2):
            here = ((z == 0) & (c == 1)) if part == 1 else ((z == 3) & (c == 0))

            @pl.when(here)
            def _(part=part):
                near2_ref[part] = last_ref[...]
                far2_ref[part] = last_far_ref[...]

            @pl.when(jnp.logical_not(here))
            def _(part=part):
                near2_ref[part] = kept_ref[2 + part]
                far2_ref[part] = far_later_ref[part]

    def rows_of(ref, p):
        return ref[0:NZ, pl.ds(p * PAIR_ROWS, PAIR_ROWS), :].reshape(P_SIZE, depth)

    def columns_of(distance, q, part, near):
        rows = pl.ds(q * PAIR_ROWS, PAIR_ROWS)
        if distance == 0:
            return (sent_ref if near else far_ref)[2 * part + c, rows, :]
        if distance == 1:
            return kept_ref[part, rows, :] if near else far_ref[NZ + part, rows, :]
        return (near2_ref if near else far2_ref)[part, rows, :]

    for p in range(2):

        @pl.when((y == p) if mine else (y != p))
        def _(p=p):
            left, left_far = rows_of(sent_ref, p), rows_of(far_ref, p)
            for part, out_ref in ((x, here_ref), (1 - x, there_ref)):
                near = jnp.concatenate([columns_of(d, q, part, True) for d, q in tiles[p]], axis=0)
                far = jnp.concatenate([columns_of(d, q, part, False) for d, q in tiles[p]], axis=0)
                total = lax.dot_general(left, near, nt, preferred_element_type=jnp.float32) + lax.dot_general(
                    left_far, far, nt, preferred_element_type=jnp.float32
                )
                out_ref[...] = total.astype(out_ref.dtype)


def plane_tiles(tiles, sent, far, kept, *last):
    columns = len(tiles[0]) * PAIR_ROWS
    part = bf16(P_SIZE, columns)
    room = (2, *sent.shape[1:])

    def half(mine):
        return call(
            functools.partial(tile_kernel, tiles, mine),
            (jax.ShapeDtypeStruct(part.shape, jnp.float32) if mine else part, part),
            [IN_VMEM] * (3 + len(last)),
            (IN_VMEM,) * 2,
            (2 * 2 * P_SIZE * columns * 2 * sent.shape[2], 8 * 1024 * 1024),
            (pltpu.VMEM(room, jnp.bfloat16),) * 2 if last else (),
        )(sent, far, kept, *last)

    (y_part, d_part), (mine, x_part) = half(False), half(True)
    return mine, y_part, d_part, x_part


def plane_shards(dosage, row_counts, assignment, center, weight):
    capacity, width = dosage.shape
    half = width // NY
    panels = NZ * NY
    slots = capacity // panels
    group_slots = 2 * slots
    group_rows = 2 * PAIR_ROWS

    center, weight = center.reshape(1, -1), weight.reshape(1, -1)
    chunk_rows = [len(chunk) * group_slots for chunk in CHUNKS]
    slot, counts, rows, away = call(
        functools.partial(first_kernel, slots),
        (
            jax.ShapeDtypeStruct((1, capacity), jnp.int32),
            jax.ShapeDtypeStruct((panels, 128), jnp.int32),
            bf16(capacity, half),
            bf16(chunk_rows[0], half),
        ),
        [IN_SMEM] + [ANYWHERE] * 4,
        (IN_VMEM,) * 4,
        (2 * chunk_rows[0] * capacity * half, 3 * capacity * width),
        (
            pltpu.VMEM((capacity,), jnp.int32),
            pltpu.VMEM((1, half), jnp.float32),
            pltpu.VMEM((1, half), jnp.float32),
            pltpu.VMEM((capacity, half), jnp.bfloat16),
            pltpu.SemaphoreType.DMA((4,)),
        ),
        FIRST_LIMIT,
    )(row_counts, assignment, center, weight, dosage)
    done = {}

    def held(name, value):
        first = [done[other] for other in AFTER.get(name, ()) if other in done]
        return lax.optimization_barrier((value, *first))[0] if first else value

    def move(name, send, value):
        with jax.named_scope(name):
            done[name] = send(held(name, value))
        return done[name]

    came = [move("y0", to_y, away)]
    own, *later = call(
        functools.partial(rest_kernel, slots),
        (bf16(capacity, half),) + tuple(bf16(n, half) for n in chunk_rows[1:]),
        [IN_VMEM] * 5,
        (IN_VMEM,) * len(CHUNKS),
        (2 * capacity * capacity * width, 3 * capacity * width),
    )(slot, rows, center, weight, dosage)
    for k, away in enumerate(later, 1):
        came.append(move("y%d" % k, to_y, away))
    pieces = {}
    z = lax.axis_index("panel") // NY

    def ends(name, value):
        pieces[name] = move(name, z_ends, value)

    def middle(name, value):
        pieces[name] = move(name, z_middle, value)

    for chunk, other in zip(CHUNKS, came):
        if pieces:
            other, _ = lax.optimization_barrier((other, merged[-1]))
        other = held("m%d" % chunk[0], other)
        merged = call(
            functools.partial(merge_kernel, slots, chunk),
            (bf16(group_rows, half),) * len(chunk),
            [IN_SMEM, IN_VMEM, IN_VMEM],
            (IN_VMEM,) * len(chunk),
            (2 * len(chunk) * group_rows * group_slots * half, 4 * group_rows * half * 2),
        )(counts, own, other)
        for step, piece in zip(chunk, merged):
            pieces["o%d" % step] = piece
            if step < NZ - 1:
                ends("a%d" % step, piece)
            middle("b%d" % step, piece)

    pieces["b0"] = held("p_b0", pieces["b0"])
    ends("a3", jnp.where((z == 0) | (z == 3), pieces["o3"], pieces["b0"]))
    pieces["a1"], pieces["b1"], _, _ = lax.optimization_barrier((pieces["a1"], pieces["b1"], pieces["a0"], pieces["b0"]))
    middle("c1", pieces["a1"])
    middle("c0", pieces["a0"])
    middle("c2", pieces["a2"])
    ends("d0", pieces["b1"])
    middle("c3", pieces["a3"])
    ends("e0", pieces["c0"])
    ends("d1", pieces["b3"])
    ends("e1", pieces["c1"])
    last = [
        move("l%d" % far, lambda value, far=far: z_last(value, far), pieces["c3"]) for far in (False, True)
    ]

    names = set()
    for plane in range(NZ):
        for r in range(3):
            g = (plane - r) % NZ
            names.add("o%d" % ORDER[plane].index(g))
            names.update(FOUND[plane][s][g] for s in range(NZ) if s != plane)
    names = sorted(names - {LAST})
    sent, sent_later, kept = call(
        functools.partial(collect_kernel, names, (0,), (1, 2)),
        (bf16(NZ + 2, group_rows, half), bf16(2, group_rows, half), bf16(NZ, group_rows, half)),
        [ANYWHERE] * len(names),
        (ANYWHERE,) * 3,
        (0, 4 * 3 * NZ * group_rows * half),
        (pltpu.SemaphoreType.DMA((3 * NZ,)),),
    )(*[pieces[name] for name in names])
    far = move("pp", to_core, sent)
    far_later = move("pp2", to_core, sent_later)
    first = plane_tiles((((1, 1), (1, 0)), ((0, 0), (1, 1))), sent, far, kept)
    second = plane_tiles((((2, 1), (2, 0)), ((1, 0), (2, 1))), sent, far, kept, *last, far_later)

    def exchanged(name, mine, y_part, d_part, x_part):
        return (
            mine,
            move(name + "y", to_y, y_part),
            move(name + "d", to_diagonal, d_part),
            move(name + "x", to_x, x_part),
        )

    first = exchanged("first_", *first)
    second = exchanged("second_", *second)

    def total(parts):
        mine, *others = parts
        for other in others:
            mine = mine + other.astype(jnp.float32)
        return mine.reshape(P_SIZE, 2, PAIR_ROWS)

    return jnp.concatenate([total(first), total(second)], axis=1) * (1.0 / math.sqrt(F))


def solution(mesh):
    in_specs = (P("panel", "feat"), P("panel"), P("panel"), P(), P())
    out_specs = P("panel", None, "feat")
    planes = mesh.shape["panel"] == NZ * NY and mesh.shape["feat"] == NX * NC
    shards = plane_shards if planes else general_shards
    return jax.shard_map(shards, mesh=mesh, in_specs=in_specs, out_specs=out_specs, check_vma=False)
```

```python
import functools
import math

import jax
import jax.numpy as jnp
from jax import lax
from jax.experimental import pallas as pl
from jax.experimental.pallas import tpu as pltpu
from jax.sharding import PartitionSpec as P

F = 4096
P_SIZE = 512
ROUNDS = 4
PAIR_ROWS = 128
NZ, NY, NX, NC = 4, 2, 2, 2
AFTER = {"a2": ("e1",), "c0": ("d0",), "c1": ("a2",), "d1": ("a3",), "first_d": ("b2", "y2", "e1",), "m2": ("a0", "b0",), "p_b0": ("a0",), "pp2": ("e1",), "second_d": ("pp2",), "second_x": ("l0",), "y2": ("y0",)}
VMEM_LIMIT = 40 * 1024 * 1024
FIRST_LIMIT = 62 * 1024 * 1024
BOTH = ("panel", "feat")
ORDER = ((2, 3, 0, 1), (3, 2, 0, 1), (3, 2, 1, 0), (0, 3, 1, 2))
LAST = "e2"
CHUNKS = ((0,), (1,), (2, 3))
FOUND = (
    {1: {3: "a0", 2: "a1", 0: "a2"}, 2: {3: "a3", 2: "d0", 0: "d1"}, 3: {0: "e0", 3: "e1", 2: "e2"}},
    {
        0: {2: "a0", 3: "a1", 0: "a2", 1: "a3"},
        2: {3: "b0", 2: "b1", 1: "b2", 0: "b3"},
        3: {0: "c0", 3: "c1", 1: "c2", 2: "c3"},
    },
    {
        3: {0: "a0", 3: "a1", 1: "a2", 2: "a3"},
        1: {3: "b0", 2: "b1", 0: "b2", 1: "b3"},
        0: {2: "c0", 3: "c1", 0: "c2", 1: "c3"},
    },
    {2: {3: "a0", 2: "a1", 1: "a2"}, 1: {3: "a3", 2: "d0", 1: "d1"}, 0: {2: "e0", 3: "e1", 1: "e2"}},
)


def shifted(value, axis, steps):
    count = lax.axis_size(axis)
    pairs = [(source, (source + steps) % count) for source in range(count)]
    return lax.ppermute(value, axis, pairs)


def tile_of(left_rows, partner):
    return lax.dot_general(
        left_rows, partner, (((1,), (1,)), ((), ())), preferred_element_type=jnp.float32
    )


def general_shards(dosage, row_counts, assignment, center, weight):
    panel_total = lax.axis_size("panel")
    feat_index = lax.axis_index("feat")
    capacity = dosage.shape[0]
    feat_width = dosage.shape[1]
    send_rows = capacity // panel_total
    feat_start = feat_index * feat_width
    center_part = lax.dynamic_slice_in_dim(center, feat_start, feat_width)
    weight_part = lax.dynamic_slice_in_dim(weight, feat_start, feat_width)
    standard = ((dosage.astype(jnp.float32) - center_part) * weight_part).astype(jnp.bfloat16)
    slot_ids = jnp.arange(capacity, dtype=jnp.int32)
    live_rows = slot_ids < row_counts[0]
    targets = jnp.arange(panel_total, dtype=jnp.int32)
    onehot = ((assignment[:, None] == targets[None, :]) & live_rows[:, None]).astype(jnp.int32)
    earlier = jnp.sum((jnp.cumsum(onehot, axis=0) - onehot) * onehot, axis=1)
    slot_index = jnp.where(live_rows, assignment * send_rows + earlier, panel_total * send_rows)
    outgoing = (
        jnp.zeros((panel_total * send_rows, feat_width), jnp.bfloat16)
        .at[slot_index]
        .set(standard, mode="drop")
    )
    outgoing = outgoing.reshape(panel_total, send_rows, feat_width)
    sent_counts = jnp.sum(onehot, axis=0).reshape(panel_total, 1)
    incoming, arrived = (
        lax.all_to_all(outgoing, "panel", split_axis=0, concat_axis=0, tiled=True),
        lax.all_to_all(sent_counts, "panel", split_axis=0, concat_axis=0, tiled=True),
    )
    arrived_rows = arrived[:, 0]
    offsets = jnp.cumsum(arrived_rows) - arrived_rows
    within = jnp.arange(send_rows, dtype=jnp.int32)
    positions = jnp.where(
        within[None, :] < arrived_rows[:, None], offsets[:, None] + within[None, :], P_SIZE
    )
    own_panel = (
        jnp.zeros((P_SIZE, feat_width), jnp.bfloat16)
        .at[positions.reshape(-1)]
        .set(incoming.reshape(-1, feat_width), mode="drop")
    )
    tile_scale = 1.0 / math.sqrt(F)
    partners = []
    for round_index in range(ROUNDS):
        partners.append(shifted(own_panel, "panel", round_index + 1))
    kinship = (
        jnp.concatenate(
            [
                lax.psum_scatter(
                    tile_of(own_panel, partner)[:, None, :], "feat", scatter_dimension=2, tiled=True
                )
                for partner in partners
            ],
            axis=1,
        )
        * tile_scale
    )
    return kinship


def hop(value, move):
    pairs = []
    for z in range(NZ):
        for y in range(NY):
            for x in range(NX):
                for c in range(NC):
                    to = move(z, y, x, c)
                    if to is not None:
                        tz, ty, tx, tc = to
                        pairs.append((((z * 2 + y) * 2 + x) * 2 + c, ((tz * 2 + ty) * 2 + tx) * 2 + tc))
    return lax.ppermute(value, BOTH, pairs)


def to_y(value):
    return hop(value, lambda z, y, x, c: (z, 1 - y, x, c))


def to_x(value):
    return hop(value, lambda z, y, x, c: (z, y, 1 - x, c))


def to_diagonal(value):
    return hop(value, lambda z, y, x, c: (z, 1 - y, 1 - x, c))


def to_core(value):
    return hop(value, lambda z, y, x, c: (z, y, x, 1 - c))


def z_ends(value):
    return hop(value, lambda z, y, x, c: (z ^ 1, y, x, c))


def z_last(value, far):
    def move(z, y, x, c):
        to = 1 - c if far else c
        receiver = 1 if z in (0, 1) else 0
        if (c if z in (0, 3) else to) == receiver:
            return z ^ 1, y, x, to
        return z, y, 1 - x, c

    return hop(value, move)


def z_middle(value):
    return hop(value, lambda z, y, x, c: (3 - z, y, x, c) if z in (1, 2) else (z, y, x, 1 - c))


def place():
    panel, feat = lax.axis_index("panel"), lax.axis_index("feat")
    return panel // NY, panel % NY, feat // NC, feat % NC


def call(kernel, out_shape, in_specs, out_specs, cost, scratch=(), limit=VMEM_LIMIT):
    return pl.pallas_call(
        kernel,
        name=kernel.func.__name__,
        out_shape=out_shape,
        in_specs=in_specs,
        out_specs=out_specs,
        scratch_shapes=scratch,
        compiler_params=pltpu.CompilerParams(vmem_limit_bytes=limit),
        cost_estimate=pl.CostEstimate(flops=cost[0], bytes_accessed=cost[1], transcendentals=0),
    )


IN_VMEM = pl.BlockSpec(memory_space=pltpu.VMEM)
IN_SMEM = pl.BlockSpec(memory_space=pltpu.SMEM)
ANYWHERE = pl.BlockSpec(memory_space=pl.ANY)
IN_HBM = pl.BlockSpec(memory_space=pltpu.HBM)


def bf16(*shape):
    return jax.ShapeDtypeStruct(shape, jnp.bfloat16)


def group_at(step):
    z, _, _, _ = place()
    group = jnp.int32(ORDER[0][step])
    for plane in range(1, NZ):
        group = jnp.where(z == plane, ORDER[plane][step], group)
    return group


def picks(slot, slots, step):
    group_rows = 2 * slots
    row = lax.broadcasted_iota(jnp.int32, (group_rows, slot.shape[1]), 0) + group_at(step) * group_rows
    return jnp.where(row == slot, 1.0, 0.0).astype(jnp.bfloat16)


def picked(pick, rows):
    return jnp.dot(pick, rows, preferred_element_type=jnp.float32).astype(jnp.bfloat16)


def columns_of_half(width, part):
    half = width // NY
    feat = lax.axis_index("feat")
    return (
        pl.ds(pl.multiple_of(part * half, half), half),
        pl.ds(pl.multiple_of(feat * width + part * half, half), half),
    )


def standard(dosage_ref, center_ref, weight_ref, part):
    columns, features = columns_of_half(dosage_ref.shape[1], part)
    rows = dosage_ref[:, columns].astype(jnp.float32)
    return ((rows - center_ref[:, features]) * weight_ref[:, features]).astype(jnp.bfloat16)


def first_kernel(
    slots,
    count_ref,
    assign_hbm,
    center_hbm,
    weight_hbm,
    dosage_hbm,
    slot_ref,
    counts_ref,
    rows_ref,
    away_ref,
    assign_ref,
    center_ref,
    weight_ref,
    dosage_ref,
    sems,
):
    capacity, half = dosage_ref.shape
    _, y, _, _ = place()
    panels = capacity // slots
    columns, features = columns_of_half(NY * half, 1 - y)
    copies = [
        pltpu.make_async_copy(assign_hbm, assign_ref, sems.at[0]),
        pltpu.make_async_copy(dosage_hbm.at[:, columns], dosage_ref, sems.at[1]),
        pltpu.make_async_copy(center_hbm.at[:, features], center_ref, sems.at[2]),
        pltpu.make_async_copy(weight_hbm.at[:, features], weight_ref, sems.at[3]),
    ]
    for copy in copies:
        copy.start()
    copies[0].wait()
    assign = assign_ref[...].reshape(1, capacity)
    lane = lax.broadcasted_iota(jnp.int32, (panels, capacity), 1)
    panel_id = lax.broadcasted_iota(jnp.int32, (panels, capacity), 0)
    live = lane < count_ref[0]
    member = (panel_id == assign) & live
    running = member.astype(jnp.int32)
    step = 1
    while step < capacity:
        running = running + jnp.where(lane >= step, pltpu.roll(running, step, 1), 0)
        step *= 2
    counts_ref[...] = jnp.broadcast_to(running[:, capacity - 1 :], counts_ref.shape)
    rank = jnp.sum(jnp.where(member, running - 1, 0), axis=0, keepdims=True)
    slot = jnp.where(live[:1], assign * slots + rank, -1)
    slot_ref[...] = slot
    for copy in copies[1:]:
        copy.wait()
    rows = dosage_ref[...].astype(jnp.float32)
    rows_ref[...] = ((rows - center_ref[...]) * weight_ref[...]).astype(jnp.bfloat16)
    at = 0
    for step in CHUNKS[0]:
        away_ref[pl.ds(at, 2 * slots), :] = picked(picks(slot, slots, step), rows_ref[...])
        at += 2 * slots


def rest_kernel(slots, slot_ref, rows_ref, center_ref, weight_ref, dosage_ref, own_ref, *away_refs):
    _, y, _, _ = place()
    group_rows = 2 * slots
    slot = slot_ref[...]
    pick = {}
    for chunk, away_ref in zip(CHUNKS[1:], away_refs):
        for k, step in enumerate(chunk):
            pick[step] = picks(slot, slots, step)
            away_ref[pl.ds(k * group_rows, group_rows), :] = picked(pick[step], rows_ref[...])
    stay = standard(dosage_ref, center_ref, weight_ref, y)
    for step in range(NZ):
        rows = pick[step] if step in pick else picks(slot, slots, step)
        own_ref[pl.ds(step * group_rows, group_rows), :] = picked(rows, stay)


def merge_kernel(slots, chunk, counts_ref, own_ref, other_ref, *out_refs):
    _, y, _, _ = place()
    row = lax.broadcasted_iota(jnp.int32, (PAIR_ROWS, slots), 0)
    slot = lax.broadcasted_iota(jnp.int32, (PAIR_ROWS, slots), 1)
    for at, (step, out_ref) in enumerate(zip(chunk, out_refs)):
        group = group_at(step)
        for k in range(2):
            n_own = counts_ref[group * 2 + k, 0]
            n_other = PAIR_ROWS - n_own
            own_at = jnp.where(y == 0, 0, n_other)
            other_at = jnp.where(y == 0, n_own, 0)
            pick_own = jnp.where((row == slot + own_at) & (slot < n_own), 1.0, 0.0).astype(jnp.bfloat16)
            pick_other = jnp.where((row == slot + other_at) & (slot < n_other), 1.0, 0.0).astype(jnp.bfloat16)
            merged = jnp.dot(
                pick_own, own_ref[pl.ds((step * 2 + k) * slots, slots), :], preferred_element_type=jnp.float32
            ) + jnp.dot(
                pick_other, other_ref[pl.ds((at * 2 + k) * slots, slots), :], preferred_element_type=jnp.float32
            )
            out_ref[pl.ds(k * PAIR_ROWS, PAIR_ROWS), :] = merged.astype(jnp.bfloat16)


def collect_kernel(names, whole, split, *refs):
    pieces = dict(zip(names, refs))
    send_ref, later_ref, keep_ref, sems = refs[len(names) :]
    z, _, _, c = place()
    for zz in range(NZ):
        for cc in range(NC):

            @pl.when((z == zz) & (c == cc))
            def _(zz=zz, cc=cc):
                copies = []
                sent = kept = 0
                for r in whole + split:
                    g = (zz - r) % NZ
                    for s in range(NZ):
                        name = "o%d" % ORDER[zz].index(g) if s == zz else FOUND[zz][s][g]
                        if r in split and s % NC == cc:
                            target = keep_ref.at[kept]
                            kept += 1
                        else:
                            room = send_ref.shape[0]
                            target = send_ref.at[sent] if sent < room else later_ref.at[sent - room]
                            sent += 1
                        if name != LAST:
                            copies.append((pieces[name], target))
                started = []
                for i, (source, target) in enumerate(copies):
                    copy = pltpu.make_async_copy(source, target, sems.at[i])
                    copy.start()
                    started.append(copy)
                for copy in started:
                    copy.wait()


def tile_kernel(tiles, mine, sent_ref, far_ref, kept_ref, *refs):
    *lasts, here_ref, there_ref = refs[:2] if len(refs) == 2 else refs[:5]
    z, y, x, c = place()
    depth = sent_ref.shape[2]
    nt = (((1,), (1,)), ((), ()))
    if lasts:
        last_ref, last_far_ref, far_later_ref = lasts
        near2_ref, far2_ref = refs[5:]
        for part in range(2):
            here = ((z == 0) & (c == 1)) if part == 1 else ((z == 3) & (c == 0))

            @pl.when(here)
            def _(part=part):
                near2_ref[part] = last_ref[...]
                far2_ref[part] = last_far_ref[...]

            @pl.when(jnp.logical_not(here))
            def _(part=part):
                near2_ref[part] = kept_ref[2 + part]
                far2_ref[part] = far_later_ref[part]

    def rows_of(ref, p):
        return ref[0:NZ, pl.ds(p * PAIR_ROWS, PAIR_ROWS), :].reshape(P_SIZE, depth)

    def columns_of(distance, q, part, near):
        rows = pl.ds(q * PAIR_ROWS, PAIR_ROWS)
        if distance == 0:
            return (sent_ref if near else far_ref)[2 * part + c, rows, :]
        if distance == 1:
            return kept_ref[part, rows, :] if near else far_ref[NZ + part, rows, :]
        return (near2_ref if near else far2_ref)[part, rows, :]

    for p in range(2):

        @pl.when((y == p) if mine else (y != p))
        def _(p=p):
            left, left_far = rows_of(sent_ref, p), rows_of(far_ref, p)
            for part, out_ref in ((x, here_ref), (1 - x, there_ref)):
                near = jnp.concatenate([columns_of(d, q, part, True) for d, q in tiles[p]], axis=0)
                far = jnp.concatenate([columns_of(d, q, part, False) for d, q in tiles[p]], axis=0)
                total = lax.dot_general(left, near, nt, preferred_element_type=jnp.float32) + lax.dot_general(
                    left_far, far, nt, preferred_element_type=jnp.float32
                )
                out_ref[...] = total.astype(out_ref.dtype)


def plane_tiles(tiles, sent, far, kept, *last):
    columns = len(tiles[0]) * PAIR_ROWS
    part = bf16(P_SIZE, columns)
    room = (2, *sent.shape[1:])

    def half(mine):
        return call(
            functools.partial(tile_kernel, tiles, mine),
            (jax.ShapeDtypeStruct(part.shape, jnp.float32) if mine else part, part),
            [IN_VMEM] * (3 + len(last)),
            (IN_VMEM,) * 2,
            (2 * 2 * P_SIZE * columns * 2 * sent.shape[2], 8 * 1024 * 1024),
            (pltpu.VMEM(room, jnp.bfloat16),) * 2 if last else (),
        )(sent, far, kept, *last)

    (y_part, d_part), (mine, x_part) = half(False), half(True)
    return mine, y_part, d_part, x_part


def plane_shards(dosage, row_counts, assignment, center, weight):
    capacity, width = dosage.shape
    half = width // NY
    panels = NZ * NY
    slots = capacity // panels
    group_slots = 2 * slots
    group_rows = 2 * PAIR_ROWS

    center, weight = center.reshape(1, -1), weight.reshape(1, -1)
    chunk_rows = [len(chunk) * group_slots for chunk in CHUNKS]
    slot, counts, rows, away = call(
        functools.partial(first_kernel, slots),
        (
            jax.ShapeDtypeStruct((1, capacity), jnp.int32),
            jax.ShapeDtypeStruct((panels, 128), jnp.int32),
            bf16(capacity, half),
            bf16(chunk_rows[0], half),
        ),
        [IN_SMEM] + [ANYWHERE] * 4,
        (IN_VMEM,) * 4,
        (2 * chunk_rows[0] * capacity * half, 3 * capacity * width),
        (
            pltpu.VMEM((capacity,), jnp.int32),
            pltpu.VMEM((1, half), jnp.float32),
            pltpu.VMEM((1, half), jnp.float32),
            pltpu.VMEM((capacity, half), jnp.bfloat16),
            pltpu.SemaphoreType.DMA((4,)),
        ),
        FIRST_LIMIT,
    )(row_counts, assignment, center, weight, dosage)
    done = {}

    def held(name, value):
        first = [done[other] for other in AFTER.get(name, ()) if other in done]
        return lax.optimization_barrier((value, *first))[0] if first else value

    def move(name, send, value):
        with jax.named_scope(name):
            done[name] = send(held(name, value))
        return done[name]

    came = [move("y0", to_y, away)]
    own, *later = call(
        functools.partial(rest_kernel, slots),
        (bf16(capacity, half),) + tuple(bf16(n, half) for n in chunk_rows[1:]),
        [IN_VMEM] * 5,
        (IN_VMEM,) * len(CHUNKS),
        (2 * capacity * capacity * width, 3 * capacity * width),
    )(slot, rows, center, weight, dosage)
    for k, away in enumerate(later, 1):
        came.append(move("y%d" % k, to_y, away))
    pieces = {}
    z = lax.axis_index("panel") // NY

    def ends(name, value):
        pieces[name] = move(name, z_ends, value)

    def middle(name, value):
        pieces[name] = move(name, z_middle, value)

    for chunk, other in zip(CHUNKS, came):
        if pieces:
            other, _ = lax.optimization_barrier((other, merged[-1]))
        other = held("m%d" % chunk[0], other)
        merged = call(
            functools.partial(merge_kernel, slots, chunk),
            (bf16(group_rows, half),) * len(chunk),
            [IN_SMEM, IN_VMEM, IN_VMEM],
            (IN_VMEM,) * len(chunk),
            (2 * len(chunk) * group_rows * group_slots * half, 4 * group_rows * half * 2),
        )(counts, own, other)
        for step, piece in zip(chunk, merged):
            pieces["o%d" % step] = piece
            if step < NZ - 1:
                ends("a%d" % step, piece)
            middle("b%d" % step, piece)

    pieces["b0"] = held("p_b0", pieces["b0"])
    ends("a3", jnp.where((z == 0) | (z == 3), pieces["o3"], pieces["b0"]))
    pieces["a1"], pieces["b1"], _, _ = lax.optimization_barrier((pieces["a1"], pieces["b1"], pieces["a0"], pieces["b0"]))
    middle("c1", pieces["a1"])
    middle("c0", pieces["a0"])
    middle("c2", pieces["a2"])
    ends("d0", pieces["b1"])
    middle("c3", pieces["a3"])
    ends("e0", pieces["c0"])
    ends("d1", pieces["b3"])
    ends("e1", pieces["c1"])
    last = [
        move("l%d" % far, lambda value, far=far: z_last(value, far), pieces["c3"]) for far in (False, True)
    ]

    names = set()
    for plane in range(NZ):
        for r in range(3):
            g = (plane - r) % NZ
            names.add("o%d" % ORDER[plane].index(g))
            names.update(FOUND[plane][s][g] for s in range(NZ) if s != plane)
    names = sorted(names - {LAST})
    sent, sent_later, kept = call(
        functools.partial(collect_kernel, names, (0,), (1, 2)),
        (bf16(NZ + 2, group_rows, half), bf16(2, group_rows, half), bf16(NZ, group_rows, half)),
        [ANYWHERE] * len(names),
        (ANYWHERE,) * 3,
        (0, 4 * 3 * NZ * group_rows * half),
        (pltpu.SemaphoreType.DMA((3 * NZ,)),),
    )(*[pieces[name] for name in names])
    far = move("pp", to_core, sent)
    far_later = move("pp2", to_core, sent_later)
    first = plane_tiles((((1, 1), (1, 0)), ((0, 0), (1, 1))), sent, far, kept)
    second = plane_tiles((((2, 1), (2, 0)), ((1, 0), (2, 1))), sent, far, kept, *last, far_later)

    def exchanged(name, mine, y_part, d_part, x_part):
        return (
            mine,
            move(name + "y", to_y, y_part),
            move(name + "d", to_diagonal, d_part),
            move(name + "x", to_x, x_part),
        )

    mine, y_part, d_part, x_part = first
    here, there = slice(0, PAIR_ROWS), slice(PAIR_ROWS, 2 * PAIR_ROWS)

    def beside(one, other):
        return jnp.concatenate([one, other], axis=1)

    def plus(one, other):
        return (one.astype(jnp.float32) + other.astype(jnp.float32)).astype(jnp.bfloat16)

    over_y = move("first_y", to_y, beside(d_part[:, there], y_part[:, there]))
    over_x = move("first_x", to_x, beside(d_part[:, here], x_part[:, here]))
    then_y = move("then_y", to_y, plus(y_part[:, here], over_x[:, here]))
    then_x = move("then_x", to_x, plus(x_part[:, there], over_y[:, here]))
    first = mine, beside(then_y, over_y[:, there]), beside(over_x[:, there], then_x)
    second = exchanged("second_", *second)

    def total(parts):
        mine, *others = parts
        for other in others:
            mine = mine + other.astype(jnp.float32)
        return mine.reshape(P_SIZE, 2, PAIR_ROWS)

    return jnp.concatenate([total(first), total(second)], axis=1) * (1.0 / math.sqrt(F))


def solution(mesh):
    in_specs = (P("panel", "feat"), P("panel"), P("panel"), P(), P())
    out_specs = P("panel", None, "feat")
    planes = mesh.shape["panel"] == NZ * NY and mesh.shape["feat"] == NX * NC
    shards = plane_shards if planes else general_shards
    return jax.shard_map(shards, mesh=mesh, in_specs=in_specs, out_specs=out_specs, check_vma=False)
```

```python
import functools
import math

import jax
import jax.numpy as jnp
from jax import lax
from jax.experimental import pallas as pl
from jax.experimental.pallas import tpu as pltpu
from jax.sharding import PartitionSpec as P

F = 4096
P_SIZE = 512
ROUNDS = 4
PAIR_ROWS = 128
NZ, NY, NX, NC = 4, 2, 2, 2
AFTER = {"a2": ("e1",), "c0": ("d0",), "c1": ("a2",), "d1": ("a3",), "first_d": ("b2", "y2", "e1",), "m2": ("a0", "b0",), "p_b0": ("a0",), "pp2": ("e1",), "second_d": ("pp2",), "second_x": ("l0",), "y2": ("y0",)}
VMEM_LIMIT = 40 * 1024 * 1024
FIRST_LIMIT = 62 * 1024 * 1024
BOTH = ("panel", "feat")
ORDER = ((2, 3, 0, 1), (3, 2, 0, 1), (3, 2, 1, 0), (0, 3, 1, 2))
LAST = "e2"
CHUNKS = ((0,), (1,), (2, 3))
FOUND = (
    {1: {3: "a0", 2: "a1", 0: "a2"}, 2: {3: "a3", 2: "d0", 0: "d1"}, 3: {0: "e0", 3: "e1", 2: "e2"}},
    {
        0: {2: "a0", 3: "a1", 0: "a2", 1: "a3"},
        2: {3: "b0", 2: "b1", 1: "b2", 0: "b3"},
        3: {0: "c0", 3: "c1", 1: "c2", 2: "c3"},
    },
    {
        3: {0: "a0", 3: "a1", 1: "a2", 2: "a3"},
        1: {3: "b0", 2: "b1", 0: "b2", 1: "b3"},
        0: {2: "c0", 3: "c1", 0: "c2", 1: "c3"},
    },
    {2: {3: "a0", 2: "a1", 1: "a2"}, 1: {3: "a3", 2: "d0", 1: "d1"}, 0: {2: "e0", 3: "e1", 1: "e2"}},
)


def shifted(value, axis, steps):
    count = lax.axis_size(axis)
    pairs = [(source, (source + steps) % count) for source in range(count)]
    return lax.ppermute(value, axis, pairs)


def tile_of(left_rows, partner):
    return lax.dot_general(
        left_rows, partner, (((1,), (1,)), ((), ())), preferred_element_type=jnp.float32
    )


def general_shards(dosage, row_counts, assignment, center, weight):
    panel_total = lax.axis_size("panel")
    feat_index = lax.axis_index("feat")
    capacity = dosage.shape[0]
    feat_width = dosage.shape[1]
    send_rows = capacity // panel_total
    feat_start = feat_index * feat_width
    center_part = lax.dynamic_slice_in_dim(center, feat_start, feat_width)
    weight_part = lax.dynamic_slice_in_dim(weight, feat_start, feat_width)
    standard = ((dosage.astype(jnp.float32) - center_part) * weight_part).astype(jnp.bfloat16)
    slot_ids = jnp.arange(capacity, dtype=jnp.int32)
    live_rows = slot_ids < row_counts[0]
    targets = jnp.arange(panel_total, dtype=jnp.int32)
    onehot = ((assignment[:, None] == targets[None, :]) & live_rows[:, None]).astype(jnp.int32)
    earlier = jnp.sum((jnp.cumsum(onehot, axis=0) - onehot) * onehot, axis=1)
    slot_index = jnp.where(live_rows, assignment * send_rows + earlier, panel_total * send_rows)
    outgoing = (
        jnp.zeros((panel_total * send_rows, feat_width), jnp.bfloat16)
        .at[slot_index]
        .set(standard, mode="drop")
    )
    outgoing = outgoing.reshape(panel_total, send_rows, feat_width)
    sent_counts = jnp.sum(onehot, axis=0).reshape(panel_total, 1)
    incoming, arrived = (
        lax.all_to_all(outgoing, "panel", split_axis=0, concat_axis=0, tiled=True),
        lax.all_to_all(sent_counts, "panel", split_axis=0, concat_axis=0, tiled=True),
    )
    arrived_rows = arrived[:, 0]
    offsets = jnp.cumsum(arrived_rows) - arrived_rows
    within = jnp.arange(send_rows, dtype=jnp.int32)
    positions = jnp.where(
        within[None, :] < arrived_rows[:, None], offsets[:, None] + within[None, :], P_SIZE
    )
    own_panel = (
        jnp.zeros((P_SIZE, feat_width), jnp.bfloat16)
        .at[positions.reshape(-1)]
        .set(incoming.reshape(-1, feat_width), mode="drop")
    )
    tile_scale = 1.0 / math.sqrt(F)
    partners = []
    for round_index in range(ROUNDS):
        partners.append(shifted(own_panel, "panel", round_index + 1))
    kinship = (
        jnp.concatenate(
            [
                lax.psum_scatter(
                    tile_of(own_panel, partner)[:, None, :], "feat", scatter_dimension=2, tiled=True
                )
                for partner in partners
            ],
            axis=1,
        )
        * tile_scale
    )
    return kinship


def hop(value, move):
    pairs = []
    for z in range(NZ):
        for y in range(NY):
            for x in range(NX):
                for c in range(NC):
                    to = move(z, y, x, c)
                    if to is not None:
                        tz, ty, tx, tc = to
                        pairs.append((((z * 2 + y) * 2 + x) * 2 + c, ((tz * 2 + ty) * 2 + tx) * 2 + tc))
    return lax.ppermute(value, BOTH, pairs)


def to_y(value):
    return hop(value, lambda z, y, x, c: (z, 1 - y, x, c))


def to_x(value):
    return hop(value, lambda z, y, x, c: (z, y, 1 - x, c))


def to_diagonal(value):
    return hop(value, lambda z, y, x, c: (z, 1 - y, 1 - x, c))


def to_core(value):
    return hop(value, lambda z, y, x, c: (z, y, x, 1 - c))


def z_ends(value):
    return hop(value, lambda z, y, x, c: (z ^ 1, y, x, c))


def z_last(value, far):
    def move(z, y, x, c):
        to = 1 - c if far else c
        receiver = 1 if z in (0, 1) else 0
        if (c if z in (0, 3) else to) == receiver:
            return z ^ 1, y, x, to
        return z, y, 1 - x, c

    return hop(value, move)


def z_middle(value):
    return hop(value, lambda z, y, x, c: (3 - z, y, x, c) if z in (1, 2) else (z, y, x, 1 - c))


def place():
    panel, feat = lax.axis_index("panel"), lax.axis_index("feat")
    return panel // NY, panel % NY, feat // NC, feat % NC


def call(kernel, out_shape, in_specs, out_specs, cost, scratch=(), limit=VMEM_LIMIT):
    return pl.pallas_call(
        kernel,
        name=kernel.func.__name__,
        out_shape=out_shape,
        in_specs=in_specs,
        out_specs=out_specs,
        scratch_shapes=scratch,
        compiler_params=pltpu.CompilerParams(vmem_limit_bytes=limit),
        cost_estimate=pl.CostEstimate(flops=cost[0], bytes_accessed=cost[1], transcendentals=0),
    )


IN_VMEM = pl.BlockSpec(memory_space=pltpu.VMEM)
IN_SMEM = pl.BlockSpec(memory_space=pltpu.SMEM)
ANYWHERE = pl.BlockSpec(memory_space=pl.ANY)
IN_HBM = pl.BlockSpec(memory_space=pltpu.HBM)


def bf16(*shape):
    return jax.ShapeDtypeStruct(shape, jnp.bfloat16)


def group_at(step):
    z, _, _, _ = place()
    group = jnp.int32(ORDER[0][step])
    for plane in range(1, NZ):
        group = jnp.where(z == plane, ORDER[plane][step], group)
    return group


def picks(slot, slots, step):
    group_rows = 2 * slots
    row = lax.broadcasted_iota(jnp.int32, (group_rows, slot.shape[1]), 0) + group_at(step) * group_rows
    return jnp.where(row == slot, 1.0, 0.0).astype(jnp.bfloat16)


def picked(pick, rows):
    return jnp.dot(pick, rows, preferred_element_type=jnp.float32).astype(jnp.bfloat16)


def columns_of_half(width, part):
    half = width // NY
    feat = lax.axis_index("feat")
    return (
        pl.ds(pl.multiple_of(part * half, half), half),
        pl.ds(pl.multiple_of(feat * width + part * half, half), half),
    )


def standard(dosage_ref, center_ref, weight_ref, part):
    columns, features = columns_of_half(dosage_ref.shape[1], part)
    rows = dosage_ref[:, columns].astype(jnp.float32)
    return ((rows - center_ref[:, features]) * weight_ref[:, features]).astype(jnp.bfloat16)


def first_kernel(
    slots,
    count_ref,
    assign_hbm,
    center_hbm,
    weight_hbm,
    dosage_hbm,
    slot_ref,
    counts_ref,
    rows_ref,
    away_ref,
    assign_ref,
    center_ref,
    weight_ref,
    dosage_ref,
    sems,
):
    capacity, half = dosage_ref.shape
    _, y, _, _ = place()
    panels = capacity // slots
    columns, features = columns_of_half(NY * half, 1 - y)
    copies = [
        pltpu.make_async_copy(assign_hbm, assign_ref, sems.at[0]),
        pltpu.make_async_copy(dosage_hbm.at[:, columns], dosage_ref, sems.at[1]),
        pltpu.make_async_copy(center_hbm.at[:, features], center_ref, sems.at[2]),
        pltpu.make_async_copy(weight_hbm.at[:, features], weight_ref, sems.at[3]),
    ]
    for copy in copies:
        copy.start()
    copies[0].wait()
    assign = assign_ref[...].reshape(1, capacity)
    lane = lax.broadcasted_iota(jnp.int32, (panels, capacity), 1)
    panel_id = lax.broadcasted_iota(jnp.int32, (panels, capacity), 0)
    live = lane < count_ref[0]
    member = (panel_id == assign) & live
    running = member.astype(jnp.int32)
    step = 1
    while step < capacity:
        running = running + jnp.where(lane >= step, pltpu.roll(running, step, 1), 0)
        step *= 2
    counts_ref[...] = jnp.broadcast_to(running[:, capacity - 1 :], counts_ref.shape)
    rank = jnp.sum(jnp.where(member, running - 1, 0), axis=0, keepdims=True)
    slot = jnp.where(live[:1], assign * slots + rank, -1)
    slot_ref[...] = slot
    for copy in copies[1:]:
        copy.wait()
    rows = dosage_ref[...].astype(jnp.float32)
    rows_ref[...] = ((rows - center_ref[...]) * weight_ref[...]).astype(jnp.bfloat16)
    at = 0
    for step in CHUNKS[0]:
        away_ref[pl.ds(at, 2 * slots), :] = picked(picks(slot, slots, step), rows_ref[...])
        at += 2 * slots


def rest_kernel(slots, slot_ref, rows_ref, center_ref, weight_ref, dosage_ref, own_ref, *away_refs):
    _, y, _, _ = place()
    group_rows = 2 * slots
    slot = slot_ref[...]
    pick = {}
    for chunk, away_ref in zip(CHUNKS[1:], away_refs):
        for k, step in enumerate(chunk):
            pick[step] = picks(slot, slots, step)
            away_ref[pl.ds(k * group_rows, group_rows), :] = picked(pick[step], rows_ref[...])
    stay = standard(dosage_ref, center_ref, weight_ref, y)
    for step in range(NZ):
        rows = pick[step] if step in pick else picks(slot, slots, step)
        own_ref[pl.ds(step * group_rows, group_rows), :] = picked(rows, stay)


def merge_kernel(slots, chunk, counts_ref, own_ref, other_ref, *out_refs):
    _, y, _, _ = place()
    row = lax.broadcasted_iota(jnp.int32, (PAIR_ROWS, slots), 0)
    slot = lax.broadcasted_iota(jnp.int32, (PAIR_ROWS, slots), 1)
    for at, (step, out_ref) in enumerate(zip(chunk, out_refs)):
        group = group_at(step)
        for k in range(2):
            n_own = counts_ref[group * 2 + k, 0]
            n_other = PAIR_ROWS - n_own
            own_at = jnp.where(y == 0, 0, n_other)
            other_at = jnp.where(y == 0, n_own, 0)
            pick_own = jnp.where((row == slot + own_at) & (slot < n_own), 1.0, 0.0).astype(jnp.bfloat16)
            pick_other = jnp.where((row == slot + other_at) & (slot < n_other), 1.0, 0.0).astype(jnp.bfloat16)
            merged = jnp.dot(
                pick_own, own_ref[pl.ds((step * 2 + k) * slots, slots), :], preferred_element_type=jnp.float32
            ) + jnp.dot(
                pick_other, other_ref[pl.ds((at * 2 + k) * slots, slots), :], preferred_element_type=jnp.float32
            )
            out_ref[pl.ds(k * PAIR_ROWS, PAIR_ROWS), :] = merged.astype(jnp.bfloat16)


def collect_kernel(names, whole, split, *refs):
    pieces = dict(zip(names, refs))
    send_ref, later_ref, keep_ref, sems = refs[len(names) :]
    z, _, _, c = place()
    for zz in range(NZ):
        for cc in range(NC):

            @pl.when((z == zz) & (c == cc))
            def _(zz=zz, cc=cc):
                copies = []
                sent = kept = 0
                for r in whole + split:
                    g = (zz - r) % NZ
                    for s in range(NZ):
                        name = "o%d" % ORDER[zz].index(g) if s == zz else FOUND[zz][s][g]
                        if r in split and s % NC == cc:
                            target = keep_ref.at[kept]
                            kept += 1
                        else:
                            room = send_ref.shape[0]
                            target = send_ref.at[sent] if sent < room else later_ref.at[sent - room]
                            sent += 1
                        if name != LAST:
                            copies.append((pieces[name], target))
                started = []
                for i, (source, target) in enumerate(copies):
                    copy = pltpu.make_async_copy(source, target, sems.at[i])
                    copy.start()
                    started.append(copy)
                for copy in started:
                    copy.wait()


def tile_kernel(tiles, mine, sent_ref, far_ref, kept_ref, *refs):
    *lasts, here_ref, there_ref = refs[:2] if len(refs) == 2 else refs[:5]
    z, y, x, c = place()
    depth = sent_ref.shape[2]
    nt = (((1,), (1,)), ((), ()))
    if lasts:
        last_ref, last_far_ref, far_later_ref = lasts
        near2_ref, far2_ref = refs[5:]
        for part in range(2):
            here = ((z == 0) & (c == 1)) if part == 1 else ((z == 3) & (c == 0))

            @pl.when(here)
            def _(part=part):
                near2_ref[part] = last_ref[...]
                far2_ref[part] = last_far_ref[...]

            @pl.when(jnp.logical_not(here))
            def _(part=part):
                near2_ref[part] = kept_ref[2 + part]
                far2_ref[part] = far_later_ref[part]

    def rows_of(ref, p):
        return ref[0:NZ, pl.ds(p * PAIR_ROWS, PAIR_ROWS), :].reshape(P_SIZE, depth)

    def columns_of(distance, q, part, near):
        rows = pl.ds(q * PAIR_ROWS, PAIR_ROWS)
        if distance == 0:
            return (sent_ref if near else far_ref)[2 * part + c, rows, :]
        if distance == 1:
            return kept_ref[part, rows, :] if near else far_ref[NZ + part, rows, :]
        return (near2_ref if near else far2_ref)[part, rows, :]

    for p in range(2):

        @pl.when((y == p) if mine else (y != p))
        def _(p=p):
            left, left_far = rows_of(sent_ref, p), rows_of(far_ref, p)
            for part, out_ref in ((x, here_ref), (1 - x, there_ref)):
                near = jnp.concatenate([columns_of(d, q, part, True) for d, q in tiles[p]], axis=0)
                far = jnp.concatenate([columns_of(d, q, part, False) for d, q in tiles[p]], axis=0)
                total = lax.dot_general(left, near, nt, preferred_element_type=jnp.float32) + lax.dot_general(
                    left_far, far, nt, preferred_element_type=jnp.float32
                )
                out_ref[...] = total.astype(out_ref.dtype)


def plane_tiles(tiles, sent, far, kept, *last):
    columns = len(tiles[0]) * PAIR_ROWS
    part = bf16(P_SIZE, columns)
    room = (2, *sent.shape[1:])

    def half(mine):
        return call(
            functools.partial(tile_kernel, tiles, mine),
            (jax.ShapeDtypeStruct(part.shape, jnp.float32) if mine else part, part),
            [IN_VMEM] * (3 + len(last)),
            (IN_VMEM,) * 2,
            (2 * 2 * P_SIZE * columns * 2 * sent.shape[2], 8 * 1024 * 1024),
            (pltpu.VMEM(room, jnp.bfloat16),) * 2 if last else (),
        )(sent, far, kept, *last)

    (y_part, d_part), (mine, x_part) = half(False), half(True)
    return mine, y_part, d_part, x_part


def plane_shards(dosage, row_counts, assignment, center, weight):
    capacity, width = dosage.shape
    half = width // NY
    panels = NZ * NY
    slots = capacity // panels
    group_slots = 2 * slots
    group_rows = 2 * PAIR_ROWS

    center, weight = center.reshape(1, -1), weight.reshape(1, -1)
    chunk_rows = [len(chunk) * group_slots for chunk in CHUNKS]
    slot, counts, rows, away = call(
        functools.partial(first_kernel, slots),
        (
            jax.ShapeDtypeStruct((1, capacity), jnp.int32),
            jax.ShapeDtypeStruct((panels, 128), jnp.int32),
            bf16(capacity, half),
            bf16(chunk_rows[0], half),
        ),
        [IN_SMEM] + [ANYWHERE] * 4,
        (IN_VMEM,) * 4,
        (2 * chunk_rows[0] * capacity * half, 3 * capacity * width),
        (
            pltpu.VMEM((capacity,), jnp.int32),
            pltpu.VMEM((1, half), jnp.float32),
            pltpu.VMEM((1, half), jnp.float32),
            pltpu.VMEM((capacity, half), jnp.bfloat16),
            pltpu.SemaphoreType.DMA((4,)),
        ),
        FIRST_LIMIT,
    )(row_counts, assignment, center, weight, dosage)
    done = {}

    def held(name, value):
        first = [done[other] for other in AFTER.get(name, ()) if other in done]
        return lax.optimization_barrier((value, *first))[0] if first else value

    def move(name, send, value):
        with jax.named_scope(name):
            done[name] = send(held(name, value))
        return done[name]

    came = [move("y0", to_y, away)]
    own, *later = call(
        functools.partial(rest_kernel, slots),
        (bf16(capacity, half),) + tuple(bf16(n, half) for n in chunk_rows[1:]),
        [IN_VMEM] * 5,
        (IN_VMEM,) * len(CHUNKS),
        (2 * capacity * capacity * width, 3 * capacity * width),
    )(slot, rows, center, weight, dosage)
    for k, away in enumerate(later, 1):
        came.append(move("y%d" % k, to_y, away))
    pieces = {}
    z = lax.axis_index("panel") // NY

    def ends(name, value):
        pieces[name] = move(name, z_ends, value)

    def middle(name, value):
        pieces[name] = move(name, z_middle, value)

    for chunk, other in zip(CHUNKS, came):
        if pieces:
            other, _ = lax.optimization_barrier((other, merged[-1]))
        other = held("m%d" % chunk[0], other)
        merged = call(
            functools.partial(merge_kernel, slots, chunk),
            (bf16(group_rows, half),) * len(chunk),
            [IN_SMEM, IN_VMEM, IN_VMEM],
            (IN_VMEM,) * len(chunk),
            (2 * len(chunk) * group_rows * group_slots * half, 4 * group_rows * half * 2),
        )(counts, own, other)
        for step, piece in zip(chunk, merged):
            pieces["o%d" % step] = piece
            if step < NZ - 1:
                ends("a%d" % step, piece)
            middle("b%d" % step, piece)

    pieces["b0"] = held("p_b0", pieces["b0"])
    ends("a3", jnp.where((z == 0) | (z == 3), pieces["o3"], pieces["b0"]))
    pieces["a1"], pieces["b1"], _, _ = lax.optimization_barrier((pieces["a1"], pieces["b1"], pieces["a0"], pieces["b0"]))
    middle("c1", pieces["a1"])
    middle("c0", pieces["a0"])
    middle("c2", pieces["a2"])
    ends("d0", pieces["b1"])
    middle("c3", pieces["a3"])
    ends("e0", pieces["c0"])
    ends("d1", pieces["b3"])
    ends("e1", pieces["c1"])
    last = [
        move("l%d" % far, lambda value, far=far: z_last(value, far), pieces["c3"]) for far in (False, True)
    ]

    names = set()
    for plane in range(NZ):
        for r in range(3):
            g = (plane - r) % NZ
            names.add("o%d" % ORDER[plane].index(g))
            names.update(FOUND[plane][s][g] for s in range(NZ) if s != plane)
    names = sorted(names - {LAST})
    sent, sent_later, kept = call(
        functools.partial(collect_kernel, names, (0,), (1, 2)),
        (bf16(NZ + 2, group_rows, half), bf16(2, group_rows, half), bf16(NZ, group_rows, half)),
        [ANYWHERE] * len(names),
        (ANYWHERE,) * 3,
        (0, 4 * 3 * NZ * group_rows * half),
        (pltpu.SemaphoreType.DMA((3 * NZ,)),),
    )(*[pieces[name] for name in names])
    far = move("pp", to_core, sent)
    far_later = move("pp2", to_core, sent_later)
    first = plane_tiles((((1, 1), (1, 0)), ((0, 0), (1, 1))), sent, far, kept)
    second = plane_tiles((((2, 1), (2, 0)), ((1, 0), (2, 1))), sent, far, kept, *last, far_later)

    def exchanged(name, mine, y_part, d_part, x_part):
        return (
            mine,
            move(name + "y", to_y, y_part),
            move(name + "d", to_diagonal, d_part),
            move(name + "x", to_x, x_part),
        )

    here, there = slice(0, PAIR_ROWS), slice(PAIR_ROWS, 2 * PAIR_ROWS)

    def beside(one, other):
        return jnp.concatenate([one, other], axis=1)

    def plus(one, other):
        return (one.astype(jnp.float32) + other.astype(jnp.float32)).astype(jnp.bfloat16)

    def passed(name, mine, y_part, d_part, x_part):
        over_y = move(name + "y", to_y, beside(d_part[:, there], y_part[:, there]))
        over_x = move(name + "x", to_x, beside(d_part[:, here], x_part[:, here]))
        then_y = move(name + "then_y", to_y, plus(y_part[:, here], over_x[:, here]))
        then_x = move(name + "then_x", to_x, plus(x_part[:, there], over_y[:, here]))
        return mine, beside(then_y, over_y[:, there]), beside(over_x[:, there], then_x)

    first = passed("first_", *first)
    second = passed("second_", *second)

    def total(parts):
        mine, *others = parts
        for other in others:
            mine = mine + other.astype(jnp.float32)
        return mine.reshape(P_SIZE, 2, PAIR_ROWS)

    return jnp.concatenate([total(first), total(second)], axis=1) * (1.0 / math.sqrt(F))


def solution(mesh):
    in_specs = (P("panel", "feat"), P("panel"), P("panel"), P(), P())
    out_specs = P("panel", None, "feat")
    planes = mesh.shape["panel"] == NZ * NY and mesh.shape["feat"] == NX * NC
    shards = plane_shards if planes else general_shards
    return jax.shard_map(shards, mesh=mesh, in_specs=in_specs, out_specs=out_specs, check_vma=False)
```

```python
import functools
import math

import jax
import jax.numpy as jnp
from jax import lax
from jax.experimental import pallas as pl
from jax.experimental.pallas import tpu as pltpu
from jax.sharding import PartitionSpec as P

F = 4096
P_SIZE = 512
ROUNDS = 4
PAIR_ROWS = 128
NZ, NY, NX, NC = 4, 2, 2, 2
AFTER = {"a2": ("e1",), "c0": ("d0",), "c1": ("a2",), "d1": ("a3",), "first_d": ("b2", "y2", "e1",), "m2": ("a0", "b0",), "p_b0": ("a0",), "pp2": ("e1",), "second_d": ("pp2",), "second_x": ("l0",), "y2": ("y0",)}
VMEM_LIMIT = 40 * 1024 * 1024
FIRST_LIMIT = 62 * 1024 * 1024
BOTH = ("panel", "feat")
ORDER = ((2, 3, 0, 1), (3, 2, 0, 1), (3, 2, 1, 0), (0, 3, 1, 2))
LAST = "e2"
CHUNKS = ((0,), (1,), (2, 3))
FOUND = (
    {1: {3: "a0", 2: "a1", 0: "a2"}, 2: {3: "a3", 2: "d0", 0: "d1"}, 3: {0: "e0", 3: "e1", 2: "e2"}},
    {
        0: {2: "a0", 3: "a1", 0: "a2", 1: "a3"},
        2: {3: "b0", 2: "b1", 1: "b2", 0: "b3"},
        3: {0: "c0", 3: "c1", 1: "c2", 2: "c3"},
    },
    {
        3: {0: "a0", 3: "a1", 1: "a2", 2: "a3"},
        1: {3: "b0", 2: "b1", 0: "b2", 1: "b3"},
        0: {2: "c0", 3: "c1", 0: "c2", 1: "c3"},
    },
    {2: {3: "a0", 2: "a1", 1: "a2"}, 1: {3: "a3", 2: "d0", 1: "d1"}, 0: {2: "e0", 3: "e1", 1: "e2"}},
)


def shifted(value, axis, steps):
    count = lax.axis_size(axis)
    pairs = [(source, (source + steps) % count) for source in range(count)]
    return lax.ppermute(value, axis, pairs)


def tile_of(left_rows, partner):
    return lax.dot_general(
        left_rows, partner, (((1,), (1,)), ((), ())), preferred_element_type=jnp.float32
    )


def general_shards(dosage, row_counts, assignment, center, weight):
    panel_total = lax.axis_size("panel")
    feat_index = lax.axis_index("feat")
    capacity = dosage.shape[0]
    feat_width = dosage.shape[1]
    send_rows = capacity // panel_total
    feat_start = feat_index * feat_width
    center_part = lax.dynamic_slice_in_dim(center, feat_start, feat_width)
    weight_part = lax.dynamic_slice_in_dim(weight, feat_start, feat_width)
    standard = ((dosage.astype(jnp.float32) - center_part) * weight_part).astype(jnp.bfloat16)
    slot_ids = jnp.arange(capacity, dtype=jnp.int32)
    live_rows = slot_ids < row_counts[0]
    targets = jnp.arange(panel_total, dtype=jnp.int32)
    onehot = ((assignment[:, None] == targets[None, :]) & live_rows[:, None]).astype(jnp.int32)
    earlier = jnp.sum((jnp.cumsum(onehot, axis=0) - onehot) * onehot, axis=1)
    slot_index = jnp.where(live_rows, assignment * send_rows + earlier, panel_total * send_rows)
    outgoing = (
        jnp.zeros((panel_total * send_rows, feat_width), jnp.bfloat16)
        .at[slot_index]
        .set(standard, mode="drop")
    )
    outgoing = outgoing.reshape(panel_total, send_rows, feat_width)
    sent_counts = jnp.sum(onehot, axis=0).reshape(panel_total, 1)
    incoming, arrived = (
        lax.all_to_all(outgoing, "panel", split_axis=0, concat_axis=0, tiled=True),
        lax.all_to_all(sent_counts, "panel", split_axis=0, concat_axis=0, tiled=True),
    )
    arrived_rows = arrived[:, 0]
    offsets = jnp.cumsum(arrived_rows) - arrived_rows
    within = jnp.arange(send_rows, dtype=jnp.int32)
    positions = jnp.where(
        within[None, :] < arrived_rows[:, None], offsets[:, None] + within[None, :], P_SIZE
    )
    own_panel = (
        jnp.zeros((P_SIZE, feat_width), jnp.bfloat16)
        .at[positions.reshape(-1)]
        .set(incoming.reshape(-1, feat_width), mode="drop")
    )
    tile_scale = 1.0 / math.sqrt(F)
    partners = []
    for round_index in range(ROUNDS):
        partners.append(shifted(own_panel, "panel", round_index + 1))
    kinship = (
        jnp.concatenate(
            [
                lax.psum_scatter(
                    tile_of(own_panel, partner)[:, None, :], "feat", scatter_dimension=2, tiled=True
                )
                for partner in partners
            ],
            axis=1,
        )
        * tile_scale
    )
    return kinship


def hop(value, move):
    pairs = []
    for z in range(NZ):
        for y in range(NY):
            for x in range(NX):
                for c in range(NC):
                    to = move(z, y, x, c)
                    if to is not None:
                        tz, ty, tx, tc = to
                        pairs.append((((z * 2 + y) * 2 + x) * 2 + c, ((tz * 2 + ty) * 2 + tx) * 2 + tc))
    return lax.ppermute(value, BOTH, pairs)


def to_y(value):
    return hop(value, lambda z, y, x, c: (z, 1 - y, x, c))


def to_x(value):
    return hop(value, lambda z, y, x, c: (z, y, 1 - x, c))


def to_diagonal(value):
    return hop(value, lambda z, y, x, c: (z, 1 - y, 1 - x, c))


def to_core(value):
    return hop(value, lambda z, y, x, c: (z, y, x, 1 - c))


def z_ends(value):
    return hop(value, lambda z, y, x, c: (z ^ 1, y, x, c))


def z_last(value, far):
    def move(z, y, x, c):
        to = 1 - c if far else c
        receiver = 1 if z in (0, 1) else 0
        if (c if z in (0, 3) else to) == receiver:
            return z ^ 1, y, x, to
        return z, y, 1 - x, c

    return hop(value, move)


def z_middle(value):
    return hop(value, lambda z, y, x, c: (3 - z, y, x, c) if z in (1, 2) else (z, y, x, 1 - c))


def place():
    panel, feat = lax.axis_index("panel"), lax.axis_index("feat")
    return panel // NY, panel % NY, feat // NC, feat % NC


def call(kernel, out_shape, in_specs, out_specs, cost, scratch=(), limit=VMEM_LIMIT):
    return pl.pallas_call(
        kernel,
        name=kernel.func.__name__,
        out_shape=out_shape,
        in_specs=in_specs,
        out_specs=out_specs,
        scratch_shapes=scratch,
        compiler_params=pltpu.CompilerParams(vmem_limit_bytes=limit),
        cost_estimate=pl.CostEstimate(flops=cost[0], bytes_accessed=cost[1], transcendentals=0),
    )


IN_VMEM = pl.BlockSpec(memory_space=pltpu.VMEM)
IN_SMEM = pl.BlockSpec(memory_space=pltpu.SMEM)
ANYWHERE = pl.BlockSpec(memory_space=pl.ANY)
IN_HBM = pl.BlockSpec(memory_space=pltpu.HBM)


def bf16(*shape):
    return jax.ShapeDtypeStruct(shape, jnp.bfloat16)


def group_at(step):
    z, _, _, _ = place()
    group = jnp.int32(ORDER[0][step])
    for plane in range(1, NZ):
        group = jnp.where(z == plane, ORDER[plane][step], group)
    return group


def picks(slot, slots, step):
    group_rows = 2 * slots
    row = lax.broadcasted_iota(jnp.int32, (group_rows, slot.shape[1]), 0) + group_at(step) * group_rows
    return jnp.where(row == slot, 1.0, 0.0).astype(jnp.bfloat16)


def picked(pick, rows):
    return jnp.dot(pick, rows, preferred_element_type=jnp.float32).astype(jnp.bfloat16)


def columns_of_half(width, part):
    half = width // NY
    feat = lax.axis_index("feat")
    return (
        pl.ds(pl.multiple_of(part * half, half), half),
        pl.ds(pl.multiple_of(feat * width + part * half, half), half),
    )


def standard(dosage_ref, center_ref, weight_ref, part):
    columns, features = columns_of_half(dosage_ref.shape[1], part)
    rows = dosage_ref[:, columns].astype(jnp.float32)
    return ((rows - center_ref[:, features]) * weight_ref[:, features]).astype(jnp.bfloat16)


def first_kernel(
    slots,
    count_ref,
    assign_hbm,
    center_hbm,
    weight_hbm,
    dosage_hbm,
    slot_ref,
    counts_ref,
    rows_ref,
    away_ref,
    assign_ref,
    center_ref,
    weight_ref,
    dosage_ref,
    sems,
):
    capacity, half = dosage_ref.shape
    _, y, _, _ = place()
    panels = capacity // slots
    columns, features = columns_of_half(NY * half, 1 - y)
    copies = [
        pltpu.make_async_copy(assign_hbm, assign_ref, sems.at[0]),
        pltpu.make_async_copy(dosage_hbm.at[:, columns], dosage_ref, sems.at[1]),
        pltpu.make_async_copy(center_hbm.at[:, features], center_ref, sems.at[2]),
        pltpu.make_async_copy(weight_hbm.at[:, features], weight_ref, sems.at[3]),
    ]
    for copy in copies:
        copy.start()
    copies[0].wait()
    assign = assign_ref[...].reshape(1, capacity)
    lane = lax.broadcasted_iota(jnp.int32, (panels, capacity), 1)
    panel_id = lax.broadcasted_iota(jnp.int32, (panels, capacity), 0)
    live = lane < count_ref[0]
    member = (panel_id == assign) & live
    running = member.astype(jnp.int32)
    step = 1
    while step < capacity:
        running = running + jnp.where(lane >= step, pltpu.roll(running, step, 1), 0)
        step *= 2
    counts_ref[...] = jnp.broadcast_to(running[:, capacity - 1 :], counts_ref.shape)
    rank = jnp.sum(jnp.where(member, running - 1, 0), axis=0, keepdims=True)
    slot = jnp.where(live[:1], assign * slots + rank, -1)
    slot_ref[...] = slot
    for copy in copies[1:]:
        copy.wait()
    rows = dosage_ref[...].astype(jnp.float32)
    rows_ref[...] = ((rows - center_ref[...]) * weight_ref[...]).astype(jnp.bfloat16)
    at = 0
    for step in CHUNKS[0]:
        away_ref[pl.ds(at, 2 * slots), :] = picked(picks(slot, slots, step), rows_ref[...])
        at += 2 * slots


def rest_kernel(slots, slot_ref, rows_ref, center_ref, weight_ref, dosage_ref, own_ref, *away_refs):
    _, y, _, _ = place()
    group_rows = 2 * slots
    slot = slot_ref[...]
    pick = {}
    for chunk, away_ref in zip(CHUNKS[1:], away_refs):
        for k, step in enumerate(chunk):
            pick[step] = picks(slot, slots, step)
            away_ref[pl.ds(k * group_rows, group_rows), :] = picked(pick[step], rows_ref[...])
    stay = standard(dosage_ref, center_ref, weight_ref, y)
    for step in range(NZ):
        rows = pick[step] if step in pick else picks(slot, slots, step)
        own_ref[pl.ds(step * group_rows, group_rows), :] = picked(rows, stay)


def merge_kernel(slots, chunk, counts_ref, own_ref, other_ref, *out_refs):
    _, y, _, _ = place()
    row = lax.broadcasted_iota(jnp.int32, (PAIR_ROWS, slots), 0)
    slot = lax.broadcasted_iota(jnp.int32, (PAIR_ROWS, slots), 1)
    for at, (step, out_ref) in enumerate(zip(chunk, out_refs)):
        group = group_at(step)
        for k in range(2):
            n_own = counts_ref[group * 2 + k, 0]
            n_other = PAIR_ROWS - n_own
            own_at = jnp.where(y == 0, 0, n_other)
            other_at = jnp.where(y == 0, n_own, 0)
            pick_own = jnp.where((row == slot + own_at) & (slot < n_own), 1.0, 0.0).astype(jnp.bfloat16)
            pick_other = jnp.where((row == slot + other_at) & (slot < n_other), 1.0, 0.0).astype(jnp.bfloat16)
            merged = jnp.dot(
                pick_own, own_ref[pl.ds((step * 2 + k) * slots, slots), :], preferred_element_type=jnp.float32
            ) + jnp.dot(
                pick_other, other_ref[pl.ds((at * 2 + k) * slots, slots), :], preferred_element_type=jnp.float32
            )
            out_ref[pl.ds(k * PAIR_ROWS, PAIR_ROWS), :] = merged.astype(jnp.bfloat16)


def collect_kernel(names, whole, split, *refs):
    pieces = dict(zip(names, refs))
    send_ref, later_ref, keep_ref, sems = refs[len(names) :]
    z, _, _, c = place()
    for zz in range(NZ):
        for cc in range(NC):

            @pl.when((z == zz) & (c == cc))
            def _(zz=zz, cc=cc):
                copies = []
                sent = kept = 0
                for r in whole + split:
                    g = (zz - r) % NZ
                    for s in range(NZ):
                        name = "o%d" % ORDER[zz].index(g) if s == zz else FOUND[zz][s][g]
                        if r in split and s % NC == cc:
                            target = keep_ref.at[kept]
                            kept += 1
                        else:
                            room = send_ref.shape[0]
                            target = send_ref.at[sent] if sent < room else later_ref.at[sent - room]
                            sent += 1
                        if name != LAST:
                            copies.append((pieces[name], target))
                started = []
                for i, (source, target) in enumerate(copies):
                    copy = pltpu.make_async_copy(source, target, sems.at[i])
                    copy.start()
                    started.append(copy)
                for copy in started:
                    copy.wait()


def tile_kernel(tiles, mine, sent_ref, far_ref, kept_ref, *refs):
    *lasts, here_ref, there_ref = refs[:2] if len(refs) == 2 else refs[:5]
    z, y, x, c = place()
    depth = sent_ref.shape[2]
    nt = (((1,), (1,)), ((), ()))
    if lasts:
        last_ref, last_far_ref, far_later_ref = lasts
        near2_ref, far2_ref = refs[5:]
        for part in range(2):
            here = ((z == 0) & (c == 1)) if part == 1 else ((z == 3) & (c == 0))

            @pl.when(here)
            def _(part=part):
                near2_ref[part] = last_ref[...]
                far2_ref[part] = last_far_ref[...]

            @pl.when(jnp.logical_not(here))
            def _(part=part):
                near2_ref[part] = kept_ref[2 + part]
                far2_ref[part] = far_later_ref[part]

    def rows_of(ref, p):
        return ref[0:NZ, pl.ds(p * PAIR_ROWS, PAIR_ROWS), :].reshape(P_SIZE, depth)

    def columns_of(distance, q, part, near):
        rows = pl.ds(q * PAIR_ROWS, PAIR_ROWS)
        if distance == 0:
            return (sent_ref if near else far_ref)[2 * part + c, rows, :]
        if distance == 1:
            return kept_ref[part, rows, :] if near else far_ref[NZ + part, rows, :]
        return (near2_ref if near else far2_ref)[part, rows, :]

    for p in range(2):

        @pl.when((y == p) if mine else (y != p))
        def _(p=p):
            left, left_far = rows_of(sent_ref, p), rows_of(far_ref, p)
            for part, out_ref in ((x, here_ref), (1 - x, there_ref)):
                near = jnp.concatenate([columns_of(d, q, part, True) for d, q in tiles[p]], axis=0)
                far = jnp.concatenate([columns_of(d, q, part, False) for d, q in tiles[p]], axis=0)
                total = lax.dot_general(left, near, nt, preferred_element_type=jnp.float32) + lax.dot_general(
                    left_far, far, nt, preferred_element_type=jnp.float32
                )
                out_ref[...] = total.astype(out_ref.dtype)


def finish_kernel(later_ref, first_ref, out_ref):
    scale = 1.0 / math.sqrt(F)
    both = jnp.concatenate([first_ref[...], later_ref[...]], axis=1) * scale
    out_ref[...] = both.reshape(P_SIZE, ROUNDS, PAIR_ROWS)


def plane_tiles(tiles, sent, far, kept, *last):
    columns = len(tiles[0]) * PAIR_ROWS
    part = bf16(P_SIZE, columns)
    room = (2, *sent.shape[1:])

    def half(mine):
        return call(
            functools.partial(tile_kernel, tiles, mine),
            (jax.ShapeDtypeStruct(part.shape, jnp.float32) if mine else part, part),
            [IN_VMEM] * (3 + len(last)),
            (IN_VMEM,) * 2,
            (2 * 2 * P_SIZE * columns * 2 * sent.shape[2], 8 * 1024 * 1024),
            (pltpu.VMEM(room, jnp.bfloat16),) * 2 if last else (),
        )(sent, far, kept, *last)

    (y_part, d_part), (mine, x_part) = half(False), half(True)
    return mine, y_part, d_part, x_part


def plane_shards(dosage, row_counts, assignment, center, weight):
    capacity, width = dosage.shape
    half = width // NY
    panels = NZ * NY
    slots = capacity // panels
    group_slots = 2 * slots
    group_rows = 2 * PAIR_ROWS

    center, weight = center.reshape(1, -1), weight.reshape(1, -1)
    chunk_rows = [len(chunk) * group_slots for chunk in CHUNKS]
    slot, counts, rows, away = call(
        functools.partial(first_kernel, slots),
        (
            jax.ShapeDtypeStruct((1, capacity), jnp.int32),
            jax.ShapeDtypeStruct((panels, 128), jnp.int32),
            bf16(capacity, half),
            bf16(chunk_rows[0], half),
        ),
        [IN_SMEM] + [ANYWHERE] * 4,
        (IN_VMEM,) * 4,
        (2 * chunk_rows[0] * capacity * half, 3 * capacity * width),
        (
            pltpu.VMEM((capacity,), jnp.int32),
            pltpu.VMEM((1, half), jnp.float32),
            pltpu.VMEM((1, half), jnp.float32),
            pltpu.VMEM((capacity, half), jnp.bfloat16),
            pltpu.SemaphoreType.DMA((4,)),
        ),
        FIRST_LIMIT,
    )(row_counts, assignment, center, weight, dosage)
    done = {}

    def held(name, value):
        first = [done[other] for other in AFTER.get(name, ()) if other in done]
        return lax.optimization_barrier((value, *first))[0] if first else value

    def move(name, send, value):
        with jax.named_scope(name):
            done[name] = send(held(name, value))
        return done[name]

    came = [move("y0", to_y, away)]
    own, *later = call(
        functools.partial(rest_kernel, slots),
        (bf16(capacity, half),) + tuple(bf16(n, half) for n in chunk_rows[1:]),
        [IN_VMEM] * 5,
        (IN_VMEM,) * len(CHUNKS),
        (2 * capacity * capacity * width, 3 * capacity * width),
    )(slot, rows, center, weight, dosage)
    for k, away in enumerate(later, 1):
        came.append(move("y%d" % k, to_y, away))
    pieces = {}
    z = lax.axis_index("panel") // NY

    def ends(name, value):
        pieces[name] = move(name, z_ends, value)

    def middle(name, value):
        pieces[name] = move(name, z_middle, value)

    for chunk, other in zip(CHUNKS, came):
        if pieces:
            other, _ = lax.optimization_barrier((other, merged[-1]))
        other = held("m%d" % chunk[0], other)
        merged = call(
            functools.partial(merge_kernel, slots, chunk),
            (bf16(group_rows, half),) * len(chunk),
            [IN_SMEM, IN_VMEM, IN_VMEM],
            (IN_VMEM,) * len(chunk),
            (2 * len(chunk) * group_rows * group_slots * half, 4 * group_rows * half * 2),
        )(counts, own, other)
        for step, piece in zip(chunk, merged):
            pieces["o%d" % step] = piece
            if step < NZ - 1:
                ends("a%d" % step, piece)
            middle("b%d" % step, piece)

    pieces["b0"] = held("p_b0", pieces["b0"])
    ends("a3", jnp.where((z == 0) | (z == 3), pieces["o3"], pieces["b0"]))
    pieces["a1"], pieces["b1"], _, _ = lax.optimization_barrier((pieces["a1"], pieces["b1"], pieces["a0"], pieces["b0"]))
    middle("c1", pieces["a1"])
    middle("c0", pieces["a0"])
    middle("c2", pieces["a2"])
    ends("d0", pieces["b1"])
    middle("c3", pieces["a3"])
    ends("e0", pieces["c0"])
    ends("d1", pieces["b3"])
    ends("e1", pieces["c1"])
    last = [
        move("l%d" % far, lambda value, far=far: z_last(value, far), pieces["c3"]) for far in (False, True)
    ]

    names = set()
    for plane in range(NZ):
        for r in range(3):
            g = (plane - r) % NZ
            names.add("o%d" % ORDER[plane].index(g))
            names.update(FOUND[plane][s][g] for s in range(NZ) if s != plane)
    names = sorted(names - {LAST})
    sent, sent_later, kept = call(
        functools.partial(collect_kernel, names, (0,), (1, 2)),
        (bf16(NZ + 2, group_rows, half), bf16(2, group_rows, half), bf16(NZ, group_rows, half)),
        [ANYWHERE] * len(names),
        (ANYWHERE,) * 3,
        (0, 4 * 3 * NZ * group_rows * half),
        (pltpu.SemaphoreType.DMA((3 * NZ,)),),
    )(*[pieces[name] for name in names])
    far = move("pp", to_core, sent)
    far_later = move("pp2", to_core, sent_later)
    first = plane_tiles((((1, 1), (1, 0)), ((0, 0), (1, 1))), sent, far, kept)
    second = plane_tiles((((2, 1), (2, 0)), ((1, 0), (2, 1))), sent, far, kept, *last, far_later)

    def exchanged(name, mine, y_part, d_part, x_part):
        return (
            mine,
            move(name + "y", to_y, y_part),
            move(name + "d", to_diagonal, d_part),
            move(name + "x", to_x, x_part),
        )

    here, there = slice(0, PAIR_ROWS), slice(PAIR_ROWS, 2 * PAIR_ROWS)

    def beside(one, other):
        return jnp.concatenate([one, other], axis=1)

    def plus(one, other):
        return (one.astype(jnp.float32) + other.astype(jnp.float32)).astype(jnp.bfloat16)

    def passed(name, mine, y_part, d_part, x_part):
        over_y = move(name + "y", to_y, beside(d_part[:, there], y_part[:, there]))
        over_x = move(name + "x", to_x, beside(d_part[:, here], x_part[:, here]))
        then_y = move(name + "then_y", to_y, plus(y_part[:, here], over_x[:, here]))
        then_x = move(name + "then_x", to_x, plus(x_part[:, there], over_y[:, here]))
        return mine, beside(then_y, over_y[:, there]), beside(over_x[:, there], then_x)

    first = passed("first_", *first)
    second = passed("second_", *second)

    def total(parts):
        mine, *others = parts
        for other in others:
            mine = mine + other.astype(jnp.float32)
        return mine

    return call(
        functools.partial(finish_kernel),
        jax.ShapeDtypeStruct((P_SIZE, ROUNDS, PAIR_ROWS), jnp.float32),
        [IN_VMEM] * 2,
        IN_VMEM,
        (8 * P_SIZE * P_SIZE, 4 * 1024 * 1024),
    )(total(second), total(first))


def solution(mesh):
    in_specs = (P("panel", "feat"), P("panel"), P("panel"), P(), P())
    out_specs = P("panel", None, "feat")
    planes = mesh.shape["panel"] == NZ * NY and mesh.shape["feat"] == NX * NC
    shards = plane_shards if planes else general_shards
    return jax.shard_map(shards, mesh=mesh, in_specs=in_specs, out_specs=out_specs, check_vma=False)
```
